128 devices in a mesh: pipe: 16 (over x, y_hi, core), dp: 8 (over z, y_lo).
Axes of the slice: x: 4, y: 4 (y_hi: 2, y_lo: 2; y = y_hi * 2 + y_lo), z: 4, core: 2. Of those that a mesh axis runs over, the one named last changes fastest.
Arguments:
- layer_input: bfloat16 [16, 2, 512, 3584], P('pipe', None, 'dp'), may hold values from -6 to 6
- residual_after: bfloat16 [16, 2, 512, 3584], P('pipe', None, 'dp'), may hold values from -6 to 6
- upstream: bfloat16 [16, 2, 512, 3584], P('pipe', None, 'dp'), may hold values from -6 to 6
- segment_lengths: int32 [16, 2, 4], P('pipe'), may hold values from 1 to 256, 512 in all within a row
- project_weight: bfloat16 [16, 3584, 8, 384], P('pipe', None, 'dp'), may hold values from -0.09375 to 0.09375
- output_weight: bfloat16 [16, 8, 128, 3584], P('pipe', 'dp'), may hold values from -0.1875 to 0.1875
- expand_weight: bfloat16 [16, 2, 2048, 3584], P('pipe', None, 'dp'), may hold values from -0.09375 to 0.09375
- reduce_weight: bfloat16 [16, 2048, 3584], P('pipe', 'dp'), may hold values from -0.125 to 0.125
Outputs:
- arriving: bfloat16 [16, 2, 512, 3584], P('pipe', None, 'dp')
- project_gradient: bfloat16 [16, 3584, 8, 384], P('pipe', None, 'dp')
- output_gradient: bfloat16 [16, 8, 128, 3584], P('pipe', 'dp')
- expand_gradient: bfloat16 [16, 2, 2048, 3584], P('pipe', None, 'dp')
- reduce_gradient: bfloat16 [16, 2048, 3584], P('pipe', 'dp')
The draws below stay inside these ranges and needn't reach their ends.
Inputs may be any that keep to these rules, and one draw needn't show every extreme that they name: `segment_lengths`: the 4 lengths of one micro-batch sum to 512; the longest is 256.
All inputs are finite; a program needn't handle non-finite values.
Results may differ from the reference program's by a relative error of at most 0.023.
Values may be sent and summed in bfloat16 or wider, within the bound.
No kernel may reach another device: no remote copies, remote signals or barrier semaphores. Data moves between devices by JAX's collectives and lax.ppermute only.
A program may use at most 192 MiB of HBM per device.

```python
import math
import jax
import jax.numpy as jnp
import numpy as np
from jax import lax

D = 3584
HD = 128
HEADS_DEV = 1
FF_DEV = 256
SEGS = 4
LAYERS = 16
HEADS = 8
FF = 2048
TOKENS = 512
N_DP = 8


def shard_levels(stream_key, extent, split, least, largest):
    level = 1.0
    for axis_at, parts in split:
        draws = jax.random.uniform(jax.random.fold_in(jax.random.fold_in(stream_key, 6), axis_at), (parts,), jnp.float32, least / len(split), largest / len(split))
        level = level * jnp.repeat(jnp.exp(draws), extent[axis_at] // parts).reshape((-1,) + (1,) * (len(extent) - 1 - axis_at))
    return level


def split_up(number_of, total, bound, lean):
    loads = [(1 << 20) // math.isqrt(rank ** lean) + 1 for rank in range(2, number_of + 1)]
    rest, counts = total - bound - (number_of - 1), [1] * (number_of - 1)
    while rest > 0:
        candidates = [i for i in range(number_of - 1) if counts[i] < bound]
        whole, budget = sum([loads[i] for i in candidates]), rest
        for i in candidates:
            more = min(bound - counts[i], max(1, budget * loads[i] // whole), rest)
            counts[i] = counts[i] + more
            rest = rest - more
    return np.array([bound] + counts)


def ragged_sizes(rng, count, total, limit, skew):
    if count == 2:
        one = jax.random.randint(rng, (), max(1, total - limit), min(limit, total - 1) + 1)
        return jnp.stack([one, total - one])
    sizes = jnp.asarray(split_up(count, total, limit, skew), jnp.int32)
    twos = (count - 1) // 2
    donor, sink = sizes[1:1 + 2 * twos:2], sizes[2:2 + 2 * twos:2]
    slack = jnp.minimum(donor - 1, limit - sink)
    passed = jax.random.randint(jax.random.fold_in(rng, 1), (twos,), 0, 1 << 20) % (slack + 1)
    sizes = sizes.at[1:1 + 2 * twos:2].set(donor - passed).at[2:2 + 2 * twos:2].set(sink + passed)
    return sizes[jax.random.permutation(jax.random.fold_in(rng, 2), count)]


def gaussian(rng, shape, scale, most, cuts=(), kind=jnp.bfloat16):
    entries = scale * jax.random.normal(rng, shape, jnp.float32)
    if cuts:
        entries = entries * shard_levels(rng, shape, cuts, -0.22, 0.18)
    return jnp.clip(entries, -most, most).astype(kind)


def setup_inputs(seed: int = 0) -> dict:
    splits = jax.random.split(jax.random.key(seed), 9)
    layer_input = gaussian(splits[0], (LAYERS, 2, TOKENS, D), 1.0, 6.0, ((0, 16), (2, 8)))
    residual_after = gaussian(splits[1], (LAYERS, 2, TOKENS, D), 1.0, 6.0, ((0, 16), (2, 8)))
    upstream = gaussian(splits[2], (LAYERS, 2, TOKENS, D), 1.0, 6.0, ((0, 16), (2, 8)))
    segment_lengths = jax.vmap(lambda own: ragged_sizes(own, SEGS, TOKENS, TOKENS // 2, 2))(jax.random.split(splits[3], LAYERS * 2)).reshape((LAYERS, 2, SEGS)).astype(jnp.int32)
    project_weight = gaussian(splits[4], (LAYERS, D, HEADS, 3 * HD), D ** -0.5, 0.09375, ((0, 16), (2, 8)))
    output_weight = gaussian(splits[5], (LAYERS, HEADS, HD, D), (HEADS * HD) ** -0.5, 0.1875, ((0, 16), (1, 8)))
    expand_weight = gaussian(splits[6], (LAYERS, 2, FF, D), D ** -0.5, 0.09375, ((0, 16), (2, 8)))
    reduce_weight = gaussian(splits[7], (LAYERS, FF, D), FF ** -0.5, 0.125, ((0, 16), (1, 8)))
    return {"layer_input": layer_input, "residual_after": residual_after, "upstream": upstream, "segment_lengths": segment_lengths, "project_weight": project_weight, "output_weight": output_weight, "expand_weight": expand_weight, "reduce_weight": reduce_weight}


EPSILON = 1e-06

def rms_scale(values):
    return lax.rsqrt(lax.optimization_barrier(jnp.mean(values * values, axis=-1, keepdims=True)) + EPSILON)

def norm_back(values, row_scale, incoming):
    cubed = row_scale * row_scale * row_scale
    return row_scale * incoming - values * cubed * lax.optimization_barrier(jnp.mean(incoming * values, axis=-1, keepdims=True))

def segment_mask(lengths, row_count):
    position = jnp.arange(row_count, dtype=jnp.int32)
    segment_ends = jnp.cumsum(lengths.astype(jnp.int32)).astype(jnp.int32)
    segment_index = lax.optimization_barrier(jnp.sum((position[:, None] >= segment_ends[None, :]).astype(jnp.int32), axis=1))
    same_doc = segment_index[:, None] == segment_index[None, :]
    return same_doc & (position[None, :] <= position[:, None])

def product(form, left, right):
    return jnp.einsum(form, left.astype(jnp.float32), right.astype(jnp.float32), precision=lax.Precision.HIGHEST)

def rounded_sum(pieces):
    lowered = pieces.astype(jnp.bfloat16)
    lowered = lax.optimization_barrier(lowered)
    return lax.optimization_barrier(jnp.sum(lowered.astype(jnp.float32), axis=0))

def layer_back(layer_rows, middle_rows, incoming, lengths, project_weight, output_weight, expand_weight, reduce_weight):
    row_count = layer_rows.shape[0]
    layer_full = layer_rows.astype(jnp.float32)
    scale_layer = rms_scale(layer_full)
    layer_norm = (layer_full * scale_layer).astype(jnp.bfloat16)
    middle_full = middle_rows.astype(jnp.float32)
    scale_middle = rms_scale(middle_full)
    middle_norm = (middle_full * scale_middle).astype(jnp.bfloat16)
    projected = product('nd,dhe->nhe', layer_norm, project_weight).astype(jnp.bfloat16)
    query_rows = projected[:, :, :HD]
    key_rows = projected[:, :, HD:2 * HD]
    value_rows = projected[:, :, 2 * HD:]
    allowed = segment_mask(lengths, row_count)
    scores = product('nhe,mhe->hnm', query_rows, key_rows) * HD ** (-0.5)
    weights = jnp.where(allowed[None], jnp.exp(scores), 0.0)
    softmax_rows = weights / lax.optimization_barrier(jnp.sum(weights, axis=-1, keepdims=True))
    softmax_low = softmax_rows.astype(jnp.bfloat16)
    attended = product('hnm,mhe->nhe', softmax_low, value_rows).astype(jnp.bfloat16)
    pair_pre = product('nd,kfd->knf', middle_norm, expand_weight)
    gate_pre = pair_pre[0]
    up_pre = pair_pre[1]
    gate_sigmoid = jax.nn.sigmoid(gate_pre)
    hidden = (gate_pre * gate_sigmoid * up_pre).astype(jnp.bfloat16)
    back_hidden = product('nd,fd->nf', incoming, reduce_weight)
    back_gate = back_hidden * up_pre * gate_sigmoid * (1.0 + gate_pre * (1.0 - gate_sigmoid))
    back_up = back_hidden * gate_pre * gate_sigmoid
    back_pair = jnp.stack([back_gate, back_up]).astype(jnp.bfloat16)
    reduce_slope = product('nf,nd->fd', hidden, incoming)
    expand_slope = product('knf,nd->kfd', back_pair, middle_norm)
    pieces = product('knpf,kpfd->pnd', back_pair.reshape(2, row_count, N_DP, FF_DEV), expand_weight.reshape(2, N_DP, FF_DEV, D))
    back_middle_norm = rounded_sum(pieces)
    back_middle = incoming.astype(jnp.float32) + norm_back(middle_full, scale_middle, back_middle_norm)
    back_middle_low = back_middle.astype(jnp.bfloat16)
    back_attended = product('nd,hed->nhe', back_middle_low, output_weight).astype(jnp.bfloat16)
    output_slope = product('nhe,nd->hed', attended, back_middle_low)
    back_softmax = product('nhe,mhe->hnm', back_attended, value_rows)
    centre = lax.optimization_barrier(jnp.sum(softmax_rows * back_softmax, axis=-1, keepdims=True))
    back_scores = (softmax_rows * (back_softmax - centre) * HD ** (-0.5)).astype(jnp.bfloat16)
    back_query = product('hnm,mhe->nhe', back_scores, key_rows)
    back_key = product('hnm,nhe->mhe', back_scores, query_rows)
    back_value = product('hnm,nhe->mhe', softmax_low, back_attended)
    back_project = jnp.concatenate([back_query, back_key, back_value], axis=-1).astype(jnp.bfloat16)
    project_slope = product('nd,nhe->dhe', layer_norm, back_project)
    pieces = product('nphe,dphe->pnd', back_project.reshape(row_count, N_DP, HEADS_DEV, 3 * HD), project_weight.reshape(D, N_DP, HEADS_DEV, 3 * HD))
    back_layer_norm = rounded_sum(pieces)
    back_input = (back_middle + norm_back(layer_full, scale_layer, back_layer_norm)).astype(jnp.bfloat16)
    return (back_input, project_slope, output_slope, expand_slope, reduce_slope)

def reference(layer_input, residual_after, upstream, segment_lengths, project_weight, output_weight, expand_weight, reduce_weight):
    leaving = []
    slopes = []
    for section_index in range(LAYERS):
        first = layer_back(layer_input[section_index, 0], residual_after[section_index, 0], upstream[section_index, 0], segment_lengths[section_index, 0], project_weight[section_index], output_weight[section_index], expand_weight[section_index], reduce_weight[section_index])
        second = layer_back(layer_input[section_index, 1], residual_after[section_index, 1], upstream[section_index, 1], segment_lengths[section_index, 1], project_weight[section_index], output_weight[section_index], expand_weight[section_index], reduce_weight[section_index])
        leaving.append((first[0], second[0]))
        slopes.append(tuple(((first[position] + second[position]).astype(jnp.bfloat16) for position in range(1, 5))))
    arriving = jnp.stack([jnp.stack([leaving[(section_index + 1) % LAYERS][0], leaving[(section_index - 1) % LAYERS][1]]) for section_index in range(LAYERS)])
    project_gradient = jnp.stack([entry[0] for entry in slopes])
    output_gradient = jnp.stack([entry[1] for entry in slopes])
    expand_gradient = jnp.stack([entry[2] for entry in slopes])
    reduce_gradient = jnp.stack([entry[3] for entry in slopes])
    return (arriving, project_gradient, output_gradient, expand_gradient, reduce_gradient)
```

```python
import jax
import jax.numpy as jnp
from jax import lax
from jax.sharding import PartitionSpec as P

EPSILON = 1e-06


def rms_scale(values):
    return lax.rsqrt(jnp.mean(values * values, axis=-1, keepdims=True) + EPSILON)


def norm_back(values, row_scale, incoming):
    cubed = row_scale * row_scale * row_scale
    return row_scale * incoming - values * cubed * jnp.mean(
        incoming * values, axis=-1, keepdims=True
    )


def shift(value, dz, dy):
    pairs = [(i, ((i // 2 + dz) % 4) * 2 + ((i % 2) ^ dy)) for i in range(8)]
    return lax.ppermute(value, "dp", pairs)


def gather_blocks(own):
    over = shift(own, 0, 1)
    below = shift(own, 1, 0)
    above = shift(own, -1, 0)
    below_over = shift(over, 1, 0)
    above_over = shift(over, -1, 0)
    far = shift(below, 1, 0)
    far_over = shift(above_over, -1, 0)
    return [[own, over], [above, above_over], [far, far_over], [below, below_over]]


def scatter_sum(parts):
    wide = lambda value: value.astype(jnp.float32)
    low = lambda value: value.astype(jnp.bfloat16)
    from_below = shift(parts[2][0], 1, 0)
    from_above = shift(parts[2][1], -1, 0)
    up_own = shift(low(wide(parts[1][0]) + wide(from_below)), 1, 0)
    up_over = shift(parts[1][1], 1, 0)
    down_own = shift(parts[3][0], -1, 0)
    down_over = shift(low(wide(parts[3][1]) + wide(from_above)), -1, 0)
    over = shift(low(wide(parts[0][1]) + wide(up_over) + wide(down_over)), 0, 1)
    return wide(parts[0][0]) + wide(up_own) + wide(down_own) + wide(over)


def blocks_of(rows):
    return [[rows[(2 * dz + dy) * 64 : (2 * dz + dy + 1) * 64] for dy in range(2)] for dz in range(4)]


def joined(blocks):
    return jnp.concatenate([blocks[dz][dy] for dz in range(4) for dy in range(2)], axis=-2)


def segment_mask(lengths, position):
    segment_ends = jnp.cumsum(lengths)
    segment_index = jnp.sum((position[:, None] >= segment_ends[None, :]).astype(jnp.int32), axis=1)
    same_doc = segment_index[:, None] == segment_index[None, :]
    return same_doc & (position[None, :] <= position[:, None])


def dot(spec, left, right):
    return jnp.einsum(spec, left, right, preferred_element_type=jnp.float32)


def on_device(
    layer_input,
    residual_after,
    upstream,
    segment_lengths,
    project_weight,
    output_weight,
    expand_weight,
    reduce_weight,
):
    rank = lax.axis_index("dp")
    z, y = rank // 2, rank % 2
    position = jnp.concatenate(
        [
            (((z + dz) % 4) * 2 + (y ^ dy)) * 64 + jnp.arange(64, dtype=jnp.int32)
            for dz in range(4)
            for dy in range(2)
        ]
    )
    project = project_weight[0, :, 0]
    output = output_weight[0, 0]
    expand = expand_weight[0].reshape(512, 3584)
    reduce = reduce_weight[0]
    pairs = [
        gather_blocks(jnp.stack([residual_after[0, slot], upstream[0, slot]])) for slot in range(2)
    ]
    layers = gather_blocks(layer_input[0])
    layers = joined(layers)
    norms, hiddens, backs, comings, leaves = [], [], [], [], []
    for slot in range(2):
        both = joined(pairs[slot])
        middle_full = both[0].astype(jnp.float32)
        incoming = both[1]
        middle_norm = (middle_full * rms_scale(middle_full)).astype(jnp.bfloat16)
        pre = dot("nd,fd->nf", middle_norm, expand)
        gate_pre, up_pre = pre[:, :256], pre[:, 256:]
        back_hidden = dot("nd,fd->nf", incoming, reduce)
        gate_sigmoid = jax.nn.sigmoid(gate_pre)
        silu = gate_pre * gate_sigmoid
        hidden = (silu * up_pre).astype(jnp.bfloat16)
        back_gate = back_hidden * up_pre * gate_sigmoid * (1.0 + gate_pre * (1.0 - gate_sigmoid))
        back_up = back_hidden * silu
        back_pair = jnp.concatenate([back_gate, back_up], axis=1).astype(jnp.bfloat16)
        branch = dot("nf,fd->nd", back_pair, expand).astype(jnp.bfloat16)
        norms.append(middle_norm)
        hiddens.append(hidden)
        backs.append(back_pair)
        comings.append(incoming)
        own_norm_back = scatter_sum(blocks_of(branch))
        own_middle = residual_after[0, slot].astype(jnp.float32)
        back_middle = upstream[0, slot].astype(jnp.float32) + norm_back(
            own_middle, rms_scale(own_middle), own_norm_back
        )
        leaves.append(back_middle)
    layer_norms, attends, lows, projects, handed = [], [], [], [], []
    for slot in range(2):
        back_middle = leaves[slot]
        back_middle_low = joined(gather_blocks(back_middle.astype(jnp.bfloat16)))
        layer_full = layers[slot].astype(jnp.float32)
        layer_norm = (layer_full * rms_scale(layer_full)).astype(jnp.bfloat16)
        projected = dot("nd,de->ne", layer_norm, project).astype(jnp.bfloat16)
        query, key, value = projected[:, :128], projected[:, 128:256], projected[:, 256:]
        allowed = segment_mask(segment_lengths[0, slot], position)
        scores = dot("ne,me->nm", query, key) * 128 ** (-0.5)
        weights = jnp.where(allowed, jnp.exp(scores), 0.0)
        softmax_rows = weights / jnp.sum(weights, axis=-1, keepdims=True)
        softmax_low = softmax_rows.astype(jnp.bfloat16)
        attended = dot("nm,me->ne", softmax_low, value).astype(jnp.bfloat16)
        back_attended = dot("nd,ed->ne", back_middle_low, output).astype(jnp.bfloat16)
        back_softmax = dot("ne,me->nm", back_attended, value)
        centre = jnp.sum(softmax_rows * back_softmax, axis=-1, keepdims=True)
        back_scores = (softmax_rows * (back_softmax - centre) * 128 ** (-0.5)).astype(jnp.bfloat16)
        back_query = dot("nm,me->ne", back_scores, key)
        back_key = dot("nm,ne->me", back_scores, query)
        back_value = dot("nm,ne->me", softmax_low, back_attended)
        back_project = jnp.concatenate([back_query, back_key, back_value], axis=-1).astype(
            jnp.bfloat16
        )
        terms = dot("ne,de->nd", back_project, project).astype(jnp.bfloat16)
        own_layer_back = scatter_sum(blocks_of(terms))
        own_layer = layer_input[0, slot].astype(jnp.float32)
        back_input = back_middle + norm_back(own_layer, rms_scale(own_layer), own_layer_back)
        step = -1 if slot == 0 else 1
        handed.append(
            lax.ppermute(
                back_input.astype(jnp.bfloat16), "pipe", [(i, (i + step) % 16) for i in range(16)]
            )
        )
        layer_norms.append(layer_norm)
        attends.append(attended)
        lows.append(back_middle_low)
        projects.append(back_project)

    def total(lefts, rights):
        left = jnp.concatenate(lefts, axis=0)
        right = jnp.concatenate(rights, axis=0)
        return dot("na,nb->ab", left, right).astype(jnp.bfloat16)

    return (
        jnp.stack(handed)[None],
        total(layer_norms, projects)[None, :, None],
        total(attends, lows)[None, None],
        total(backs, norms).reshape(1, 2, 256, 3584),
        total(hiddens, comings)[None],
    )


def solution(mesh):
    return jax.shard_map(
        on_device,
        mesh=mesh,
        in_specs=(
            P("pipe", None, "dp", None),
            P("pipe", None, "dp", None),
            P("pipe", None, "dp", None),
            P("pipe", None, None),
            P("pipe", None, "dp", None),
            P("pipe", "dp", None, None),
            P("pipe", None, "dp", None),
            P("pipe", "dp", None),
        ),
        out_specs=(
            P("pipe", None, "dp", None),
            P("pipe", None, "dp", None),
            P("pipe", "dp", None, None),
            P("pipe", None, "dp", None),
            P("pipe", "dp", None),
        ),
        check_vma=False,
    )
```

```python
import functools

import jax
import jax.numpy as jnp
from jax import lax
from jax.experimental import pallas as pl
from jax.experimental.pallas import tpu as pltpu
from jax.sharding import PartitionSpec as P

EPSILON = 1e-06
D = 3584
BLOCK = 64
PAIR = 2 * BLOCK
TOKENS = 512
FF = 256
HEAD = 128
TILE = 512
TILES = D // TILE
BF16 = jnp.bfloat16
F32 = jnp.float32

ANY = pl.BlockSpec(memory_space=pl.ANY)
HBM = pl.BlockSpec(memory_space=pltpu.HBM)
VMEM = pl.BlockSpec(memory_space=pltpu.VMEM)
SMEM = pl.BlockSpec(memory_space=pltpu.SMEM)


def rms_scale(values):
    return lax.rsqrt(jnp.mean(values * values, axis=-1, keepdims=True) + EPSILON)


def norm_back(values, row_scale, incoming):
    cubed = row_scale * row_scale * row_scale
    return row_scale * incoming - values * cubed * jnp.mean(
        incoming * values, axis=-1, keepdims=True
    )


def dot_nn(left, right):
    return lax.dot_general(left, right, (((1,), (0,)), ((), ())), preferred_element_type=F32)


def dot_nt(left, right):
    return lax.dot_general(left, right, (((1,), (1,)), ((), ())), preferred_element_type=F32)


def dot_tn(left, right):
    return lax.dot_general(left, right, (((0,), (0,)), ((), ())), preferred_element_type=F32)


def shape(*dims, dtype=BF16):
    return jax.ShapeDtypeStruct(dims, dtype)


def params():
    return pltpu.CompilerParams(vmem_limit_bytes=62 * 1024 * 1024)


def cost(long=True):
    return pl.CostEstimate(
        flops=10**12 if long else 0, bytes_accessed=10**10 if long else 0, transcendentals=0
    )


def listed(earlier):
    return list(earlier) if isinstance(earlier, (list, tuple)) else [earlier]


def rows_at(start, count):
    if not isinstance(start, int):
        start = pl.multiple_of(start, BLOCK)
    return pl.ds(start, count)


def block_rows(dz, y):
    return rows_at((2 * dz + y) * BLOCK, BLOCK)


def shift(value, dz, dy):
    pairs = [(i, ((i // 2 + dz) % 4) * 2 + ((i % 2) ^ dy)) for i in range(8)]
    return lax.ppermute(value, "dp", pairs)


def one_way(value, source):
    return lax.ppermute(value, "dp", [(2 * z + source, 2 * z + 1 - source) for z in range(4)])


def small(arrays, loads, outs, earlier, body=None, place=None, long=True):
    earlier = listed(earlier)
    plans = [loads(0)] if place is None else [loads(0), loads(1)]
    buffers = {}
    for number, _, rows, buffer, at in plans[0] + plans[-1]:
        old = buffers.get(buffer, ((0,), None))[0]
        dims = (max(old[0], at + rows), arrays[number].shape[-1])
        buffers[buffer] = (dims, arrays[number].dtype)
    for out, buffer in outs:
        buffers[buffer] = (out.shape, out.dtype)
    names = sorted(buffers)
    n_place = 0 if place is None else 1

    def kernel(*refs):
        sources = refs[n_place : n_place + len(arrays)]
        refs_left = refs[n_place + len(arrays) + len(earlier) :]
        targets = refs_left[: len(outs)]
        held = dict(zip(names, refs_left[len(outs) :]))
        in_sem, out_sem = refs[-2:]

        def copies_of(plan):
            return [
                pltpu.make_async_copy(
                    sources[number].at[index],
                    held[buffer].at[pl.ds(at, rows)],
                    in_sem.at[n],
                )
                for n, (number, index, rows, buffer, at) in enumerate(plan)
            ]

        if place is None:
            for copy in copies_of(plans[0]):
                copy.start()
            for copy in copies_of(plans[0]):
                copy.wait()
        else:
            for y in range(2):

                @pl.when(refs[0][1] == y)
                def _(y=y):
                    for copy in copies_of(plans[y]):
                        copy.start()
                    for copy in copies_of(plans[y]):
                        copy.wait()

        if body is not None:
            body(held, None if place is None else refs[0])
        copies = [
            pltpu.make_async_copy(held[buffer], target, out_sem.at[n])
            for n, ((_, buffer), target) in enumerate(zip(outs, targets))
        ]
        for copy in copies:
            copy.start()
        for copy in copies:
            copy.wait()

    return pl.pallas_call(
        kernel,
        out_shape=tuple(out for out, _ in outs),
        in_specs=[SMEM] * n_place + [HBM] * len(arrays) + [ANY] * len(earlier),
        out_specs=(HBM,) * len(outs),
        scratch_shapes=[pltpu.VMEM(*buffers[k]) for k in names]
        + [pltpu.SemaphoreType.DMA((len(plans[0]),)), pltpu.SemaphoreType.DMA((len(outs),))],
        compiler_params=params(),
        cost_estimate=cost(long),
    )(*([] if place is None else [place]), *arrays, *earlier)


def first_rows(start, rows):
    return (pl.ds(start, rows),)


def wide(ref):
    return ref[...].astype(F32)


def stacked(arrays, earlier):
    def loads(_):
        return [(n, (0, slot), BLOCK, "all", n * BLOCK) for n, (_, slot) in enumerate(arrays)]

    outs = [(shape(len(arrays) * BLOCK, D), "all")]
    return small([array for array, _ in arrays], loads, outs, earlier)


def gather_blocks(own, over=None):
    over = shift(own, 0, 1) if over is None else over
    below = shift(own, 1, 0)
    above = shift(own, -1, 0)
    below_over = shift(over, 1, 0)
    above_over = shift(over, -1, 0)
    far = shift(below, 1, 0)
    far_over = shift(above_over, -1, 0)
    return {
        (0, 0): own,
        (0, 1): over,
        (1, 0): above,
        (1, 1): above_over,
        (2, 0): far,
        (2, 1): far_over,
        (3, 0): below,
        (3, 1): below_over,
    }


def gather_column(own, earlier, both, long=True):
    below, above = shift(own, 1, 0), shift(own, -1, 0)

    def loads(_):
        return [
            (0, first_rows(0, BLOCK), BLOCK, "a", 0),
            (1, first_rows(BLOCK, BLOCK), BLOCK, "b", 0),
            (1, first_rows(0, PAIR), PAIR, "sides", 0),
            (0, first_rows(0, PAIR), PAIR, "sides", PAIR),
        ][: 4 if both else 2]

    outs = [(shape(BLOCK, D), "a"), (shape(BLOCK, D), "b"), (shape(2 * PAIR, D), "sides")]
    made = small([below, above], loads, outs[: 3 if both else 2], earlier, long=long)
    return (own, above, shift(made[0], 1, 0), shift(made[1], -1, 0), below), made[-1]


def term_near(terms, far, earlier, long=True):
    def loads(_):
        return [
            (0, first_rows(0, PAIR), PAIR, "up", 0),
            (1, first_rows(0, PAIR), PAIR, "down", 0),
            (2, first_rows(0, BLOCK), BLOCK, "a", 0),
            (3, first_rows(0, BLOCK), BLOCK, "b", 0),
        ]

    def body(held, _):
        up, down = held["up"], held["down"]
        up[:BLOCK] = (up[:BLOCK].astype(F32) + wide(held["a"])).astype(BF16)
        down[BLOCK:] = (down[BLOCK:].astype(F32) + wide(held["b"])).astype(BF16)

    outs = [(shape(PAIR, D), "up"), (shape(PAIR, D), "down")]
    up, down = small([terms[0], terms[1], *far], loads, outs, earlier, body, long=long)
    return (shift(up, 1, 0), shift(down, -1, 0)), up


def term_sum(term, near, earlier, long=True):
    def loads(_):
        whole = first_rows(0, PAIR)
        return [(0, whole, PAIR, "a", 0), (1, whole, PAIR, "b", 0), (2, whole, PAIR, "c", 0)]

    def body(held, _):
        held["a"][...] = (wide(held["a"]) + wide(held["b"]) + wide(held["c"])).astype(BF16)

    return small([term, *near], loads, [(shape(PAIR, D), "a")], earlier, body, long=long)


def branch_middle(terms, own, over, place, earlier):
    count = len(terms[0])

    def loads(y):
        first, second = 2 * count + 2 * y, 2 * count + 2 * y + 1
        if y == 1:
            first, second = second, first
        found = [
            (count * y + n, first_rows(0, PAIR), PAIR, f"term{n}", 0) for n in range(count)
        ]
        return found + [
            (first, first_rows(0, BLOCK), BLOCK, "values", 0),
            (second, first_rows(0, BLOCK), BLOCK, "values", BLOCK),
            (first, first_rows(BLOCK, BLOCK), BLOCK, "coming", 0),
            (second, first_rows(BLOCK, BLOCK), BLOCK, "coming", BLOCK),
        ]

    def body(held, _):
        for start in (0, BLOCK):
            rows = pl.ds(start, BLOCK)
            part = lambda name: held[name][rows].astype(F32)
            total = sum(part(f"term{n}") for n in range(count))
            values = part("values")
            result = part("coming") + norm_back(values, rms_scale(values), total)
            held["wide"][rows] = result
            held["coming"][rows] = result.astype(BF16)

    outs = [(shape(PAIR, D, dtype=F32), "wide"), (shape(PAIR, D), "coming")]
    arrays = [*terms[0], *terms[1], own[0], over[0], own[1], over[1]]
    return small(arrays, loads, outs, earlier, body, place)


def back_input(term, near, layers, back_middle, place, earlier):
    def loads(_):
        names = ("term", "up", "down", "values", "wide")
        return [(n, first_rows(0, PAIR), PAIR, name, 0) for n, name in enumerate(names)]

    def body(held, place_ref):
        for start in (0, BLOCK):
            rows = pl.ds(start, BLOCK)
            part = lambda name: held[name][rows].astype(F32)
            total = part("term") + part("up") + part("down")
            values = part("values")
            result = part("wide") + norm_back(values, rms_scale(values), total)
            held["up"][rows] = result.astype(BF16)
        for y in range(2):

            @pl.when(place_ref[1] == y)
            def _(y=y):
                held["keep"][...] = held["up"][y * BLOCK : (y + 1) * BLOCK]
                held["cross"][...] = held["up"][(1 - y) * BLOCK : (2 - y) * BLOCK]

    outs = [(shape(BLOCK, D), "keep"), (shape(BLOCK, D), "cross")]
    return small([term, *near, layers, back_middle], loads, outs, earlier, body, place)


def second_slot(residual, upstream, layer, place, earlier):
    def loads(y):
        return [
            (0, (0, 1), BLOCK, "own", 0),
            (1, (0, 1), BLOCK, "own", BLOCK),
            (2, (0, 1 - y), BLOCK, "sent", 0),
            (2, (0, y), BLOCK, "kept", 0),
        ]

    outs = [(shape(PAIR, D), "own"), (shape(BLOCK, D), "sent"), (shape(BLOCK, D), "kept")]
    return small([residual, upstream, layer], loads, outs, earlier, None, place, False)


def copies(arrays, earlier):
    def loads(_):
        return [
            (n, first_rows(0, array.shape[0]), array.shape[0], f"copy{n}", 0)
            for n, array in enumerate(arrays)
        ]

    outs = [(shape(*array.shape), f"copy{n}") for n, array in enumerate(arrays)]
    return small(arrays, loads, outs, earlier, long=False)


def layer_pair(kept, other, place, earlier, long=True):
    def loads(y):
        return [
            (0, first_rows(0, BLOCK), BLOCK, "rows", y * BLOCK),
            (1, first_rows(0, BLOCK), BLOCK, "rows", (1 - y) * BLOCK),
        ]

    def body(held, _):
        for start in (0, BLOCK):
            rows = pl.ds(start, BLOCK)
            values = held["rows"][rows].astype(F32)
            held["norm"][rows] = (values * rms_scale(values)).astype(BF16)

    outs = [(shape(PAIR, D), "rows"), (shape(PAIR, D), "norm")]
    return small([kept, other], loads, outs, earlier, body, place, long)


BLOCKS = [(dz, dy) for dz in range(4) for dy in range(2)]


PIECES = (shape(PAIR, D), shape(PAIR, D), shape(BLOCK, D), shape(BLOCK, D), shape(PAIR, D))
PIECE_ROWS = ((0, PAIR), (PAIR, PAIR), (2 * PAIR, BLOCK), (2 * PAIR + BLOCK, BLOCK), (3 * PAIR, PAIR))


def store_pieces(terms, targets, cols, sem, t):
    copies = []
    for k, target in enumerate(targets):
        copies.append(
            pltpu.make_async_copy(
                terms.at[pl.ds(*PIECE_ROWS[k]), cols], target.at[:, cols], sem.at[5 * t + k]
            )
        )
        copies[-1].start()
    return copies


def feed_kernel(count, skip, *refs):
    place, pieces, refs = refs[0], refs[1 : 1 + count], refs[1 + count :]
    expand_in, reduce_in, refs = refs[0], refs[1], refs[2 + skip :]
    norm_out, coming_out, hidden_out, pair_out, *refs = refs
    targets, refs = refs[:5], refs[5:]
    middle, coming, norm, terms, expand, reduce, in_sem, coming_sem, out_sem, term_sem = refs
    z, y = place[0], place[1]

    def piece(k, part):
        if count == 8:
            return pieces[k].at[pl.ds(part * BLOCK, BLOCK)]
        dz, dy = BLOCKS[k]
        return pieces[0].at[rows_at(((z + dz) & 3) * 2 * PAIR + dy * PAIR + part * BLOCK, BLOCK)]

    def load(part, target, sem):
        return [
            pltpu.make_async_copy(
                piece(k, part),
                target.at[block_rows(dz, y ^ dy)],
                sem.at[k],
            )
            for k, (dz, dy) in enumerate(BLOCKS)
        ]

    copies = load(0, middle, in_sem)
    expand_copy = pltpu.make_async_copy(expand_in, expand, in_sem.at[8])
    coming_copies = load(1, coming, coming_sem)
    reduce_copy = pltpu.make_async_copy(reduce_in, reduce, coming_sem.at[8])
    for copy in copies + [expand_copy] + coming_copies + [reduce_copy]:
        copy.start()
    for dz in range(4):
        copies[2 * dz].wait()
        copies[2 * dz + 1].wait()
        for side in range(2):
            rows = block_rows(dz, side)
            values = middle[rows, :].astype(F32)
            norm[rows, :] = (values * rms_scale(values)).astype(BF16)
    norm_copy = pltpu.make_async_copy(norm, norm_out, out_sem.at[0])
    norm_copy.start()
    expand_copy.wait()
    pre = dot_nt(norm[...], expand[...])
    for copy in coming_copies:
        copy.wait()
    coming_copy = pltpu.make_async_copy(coming, coming_out, out_sem.at[1])
    coming_copy.start()
    reduce_copy.wait()
    back_hidden = dot_nt(coming[...], reduce[...])
    gate_pre, up_pre = pre[:, :FF], pre[:, FF:]
    gate_sigmoid = jax.nn.sigmoid(gate_pre)
    silu = gate_pre * gate_sigmoid
    hidden_out[...] = (silu * up_pre).astype(BF16)
    back_gate = back_hidden * up_pre * gate_sigmoid * (1.0 + gate_pre * (1.0 - gate_sigmoid))
    pair_out[:, :FF] = back_gate.astype(BF16)
    pair_out[:, FF:] = (back_hidden * silu).astype(BF16)
    out_copies = [norm_copy, coming_copy]
    for t in range(TILES):
        cols = pl.ds(t * TILE, TILE)
        terms[:, cols] = dot_nn(pair_out[...], expand[:, cols]).astype(BF16)
        out_copies += store_pieces(terms, targets, cols, term_sem, t)
    for copy in out_copies:
        copy.wait()


def feed_forward(place, blocks, expand, reduce, earlier, long=True):
    rows, count, earlier = (TOKENS, D), len(blocks), listed(earlier)
    return pl.pallas_call(
        functools.partial(feed_kernel, count, len(earlier)),
        out_shape=(
            shape(*rows),
            shape(*rows),
            shape(TOKENS, FF),
            shape(TOKENS, 2 * FF),
            *PIECES,
        ),
        in_specs=[SMEM] + [HBM] * (2 + count) + [ANY] * len(earlier),
        out_specs=(HBM, HBM, VMEM, VMEM) + (HBM,) * 5,
        scratch_shapes=[pltpu.VMEM(rows, BF16)] * 4
        + [
            pltpu.VMEM((2 * FF, D), BF16),
            pltpu.VMEM((FF, D), BF16),
            pltpu.SemaphoreType.DMA((9,)),
            pltpu.SemaphoreType.DMA((9,)),
            pltpu.SemaphoreType.DMA((2,)),
            pltpu.SemaphoreType.DMA((5 * TILES,)),
        ],
        compiler_params=params(),
        cost_estimate=cost(long),
    )(place, *blocks, expand, reduce, *earlier)


def load_pieces(pieces, rows, sem):
    copies = [
        pltpu.make_async_copy(pieces[k], rows.at[pl.ds(*PIECE_ROWS[k])], sem.at[k])
        for k in range(5)
    ]
    for copy in copies:
        copy.start()
    return copies


def attend_kernel(*refs):
    (place, lengths), pieces, (project0, project1, *_) = refs[:2], refs[2:7], refs[7:11]
    far_out, heads_out, soft_out, attended_out = refs[11:15]
    norm, project, in_sem, project_sem, out_sem = refs[15:]
    z, y = place[0], place[1]
    project_copies = [
        pltpu.make_async_copy(project0, project.at[0], project_sem.at[0]),
        pltpu.make_async_copy(project1, project.at[1], project_sem.at[1]),
    ]
    copies = load_pieces(pieces, norm, in_sem)
    for copy in project_copies:
        copy.start()
    for copy in copies:
        copy.wait()
    far_copy = pltpu.make_async_copy(norm.at[pl.ds(2 * PAIR, PAIR)], far_out, out_sem)
    far_copy.start()

    def position_of(dims, axis):
        index = lax.broadcasted_iota(jnp.int32, dims, axis)
        block = index >> 6
        return (((z + (block >> 1)) & 3) * 2 + (block & 1)) * BLOCK + (index & 63)

    def segment_of(position):
        end = lengths[y, 0]
        total = (position >= end).astype(jnp.int32)
        for k in (1, 2, 3):
            end = end + lengths[y, k]
            total = total + (position >= end).astype(jnp.int32)
        return total

    row, column = position_of((TOKENS, 1), 0), position_of((1, TOKENS), 1)
    allowed = (segment_of(row) == segment_of(column)) & (column <= row)
    for h in range(2):
        project_copies[h].wait()
        heads = dot_nn(norm[...], project[h]).astype(BF16)
        heads_out[h] = heads
        query, key, value = heads[:, :HEAD], heads[:, HEAD : 2 * HEAD], heads[:, 2 * HEAD :]
        scores = dot_nt(query, key) * HEAD ** (-0.5)
        weights = jnp.where(allowed, jnp.exp(scores), 0.0)
        soft = weights / jnp.sum(weights, axis=-1, keepdims=True)
        soft_out[h] = soft
        attended = dot_nn(soft.astype(BF16), value).astype(BF16)
        attended_out[:, h * HEAD : (h + 1) * HEAD] = attended
    far_copy.wait()


def attend(place, lengths, pieces, projects, earlier):
    return pl.pallas_call(
        attend_kernel,
        out_shape=(
            shape(PAIR, D),
            shape(2, TOKENS, 3 * HEAD),
            shape(2, TOKENS, TOKENS, dtype=F32),
            shape(TOKENS, 2 * HEAD),
        ),
        in_specs=[SMEM, SMEM] + [HBM] * 7 + [ANY] * 2,
        out_specs=(HBM, VMEM, VMEM, VMEM),
        scratch_shapes=[
            pltpu.VMEM((TOKENS, D), BF16),
            pltpu.VMEM((2, D, 3 * HEAD), BF16),
            pltpu.SemaphoreType.DMA((5,)),
            pltpu.SemaphoreType.DMA((2,)),
            pltpu.SemaphoreType.DMA,
        ],
        compiler_params=params(),
        cost_estimate=cost(),
    )(place, lengths, *pieces, *projects, *earlier)


def back_kernel(*refs):
    pieces, (heads, soft_in, out0, out1, project0, project1, _) = refs[:5], refs[5:12]
    middle_out, back0, back1, targets = *refs[12:15], refs[15:20]
    middle, terms, project, in_sem, project_sem, out_sem, term_sem = refs[20:]
    copies = load_pieces(pieces, middle, in_sem)
    project_copies = [
        pltpu.make_async_copy(project0, project.at[0], project_sem.at[0]),
        pltpu.make_async_copy(project1, project.at[1], project_sem.at[1]),
    ]
    for copy in project_copies:
        copy.start()
    for copy in copies:
        copy.wait()
    middle_copy = pltpu.make_async_copy(middle, middle_out, out_sem)
    middle_copy.start()
    for h, (output, back_out) in enumerate(((out0, back0), (out1, back1))):
        back_attended = dot_nt(middle[...], output[...]).astype(BF16)
        head = heads[h]
        query, key, value = head[:, :HEAD], head[:, HEAD : 2 * HEAD], head[:, 2 * HEAD :]
        soft = soft_in[h]
        back_soft = dot_nt(back_attended, value)
        centre = jnp.sum(soft * back_soft, axis=-1, keepdims=True)
        back_scores = (soft * (back_soft - centre) * HEAD ** (-0.5)).astype(BF16)
        back_out[:, :HEAD] = dot_nn(back_scores, key).astype(BF16)
        back_out[:, HEAD : 2 * HEAD] = dot_tn(back_scores, query).astype(BF16)
        back_out[:, 2 * HEAD :] = dot_tn(soft.astype(BF16), back_attended).astype(BF16)
    for copy in project_copies:
        copy.wait()
    out_copies = [middle_copy]
    for t in range(TILES):
        cols = pl.ds(t * TILE, TILE)
        total = dot_nt(back0[...], project[0, cols, :]) + dot_nt(back1[...], project[1, cols, :])
        terms[:, cols] = total.astype(BF16)
        out_copies += store_pieces(terms, targets, cols, term_sem, t)
    for copy in out_copies:
        copy.wait()


def attend_back(pieces, heads, soft, outputs, projects, earlier, long=True):
    back = shape(TOKENS, 3 * HEAD)
    return pl.pallas_call(
        back_kernel,
        out_shape=(shape(TOKENS, D), back, back, *PIECES),
        in_specs=[HBM] * 5 + [VMEM] * 4 + [HBM] * 2 + [ANY],
        out_specs=(HBM, VMEM, VMEM) + (HBM,) * 5,
        scratch_shapes=[pltpu.VMEM((TOKENS, D), BF16)] * 2
        + [
            pltpu.VMEM((2, D, 3 * HEAD), BF16),
            pltpu.SemaphoreType.DMA((5,)),
            pltpu.SemaphoreType.DMA((2,)),
            pltpu.SemaphoreType.DMA,
            pltpu.SemaphoreType.DMA((5 * TILES,)),
        ],
        compiler_params=params(),
        cost_estimate=cost(long),
    )(*pieces, heads, soft, *outputs, *projects, earlier)


def fixed(*dims):
    return pl.BlockSpec(dims, lambda t: (0, 0))


def column_tile(rows):
    return pl.BlockSpec((rows, TILE), lambda t: (0, t))


def row_tile(columns):
    return pl.BlockSpec((TILE, columns), lambda t: (t, 0))


def gradient(lefts, rights, earlier, flip=False, long=True):
    rows, columns = lefts[0].shape[1], rights[0].shape[1]
    earlier = listed(earlier)

    def kernel(left0, right0, left1, right1, *refs):
        total = dot_tn(left0[...], right0[...]) + dot_tn(left1[...], right1[...])
        refs[-1][...] = total.astype(BF16)

    if flip:
        left, right, out = column_tile(TOKENS), fixed(TOKENS, columns), row_tile(columns)
    else:
        left, right, out = fixed(TOKENS, rows), column_tile(TOKENS), column_tile(rows)
    return pl.pallas_call(
        kernel,
        grid=(TILES,),
        out_shape=shape(rows, columns),
        in_specs=[left, right, left, right] + [ANY] * len(earlier),
        out_specs=out,
        compiler_params=params(),
        cost_estimate=cost(long),
    )(lefts[0], rights[0], lefts[1], rights[1], *earlier)


def project_kernel(own0, far0, sides0, back0, own1, far1, sides1, back1, _, out):
    left0 = jnp.concatenate([own0[...], sides0[:PAIR], far0[...], sides0[PAIR:]])
    left1 = jnp.concatenate([own1[...], sides1[:PAIR], far1[...], sides1[PAIR:]])
    out[...] = (dot_tn(left0, back0[...]) + dot_tn(left1, back1[...])).astype(BF16)


def project_gradient(norms, backs, earlier):
    pair, sides, back = column_tile(PAIR), column_tile(2 * PAIR), fixed(TOKENS, 3 * HEAD)
    return pl.pallas_call(
        project_kernel,
        grid=(TILES,),
        out_shape=shape(D, 3 * HEAD),
        in_specs=[pair, pair, sides, back] * 2 + [ANY],
        out_specs=row_tile(3 * HEAD),
        compiler_params=params(),
        cost_estimate=cost(),
    )(*norms[0], backs[0], *norms[1], backs[1], earlier)


def output_kernel(attended, middle, _, own_out, other_out):
    total = dot_tn(attended[...], middle[...])
    own_out[...] = total[:HEAD]
    other_out[...] = total[HEAD:].astype(BF16)


def output_terms(attended, middle, earlier, long=True):
    return pl.pallas_call(
        output_kernel,
        grid=(TILES,),
        out_shape=(shape(HEAD, D, dtype=F32), shape(HEAD, D)),
        in_specs=[fixed(TOKENS, 2 * HEAD), column_tile(TOKENS), ANY],
        out_specs=(column_tile(HEAD), column_tile(HEAD)),
        compiler_params=params(),
        cost_estimate=cost(long),
    )(attended, middle, earlier)


def output_sum(own, other, earlier):
    def loads(_):
        whole = first_rows(0, HEAD)
        return [(0, whole, HEAD, "own", 0), (1, whole, HEAD, "other", 0)]

    def body(held, _):
        held["other"][...] = (held["own"][...] + wide(held["other"])).astype(BF16)

    return small([own, other], loads, [(shape(HEAD, D), "other")], earlier, body)[0]


def hand_on(value, cross):
    pairs = []
    for section in range(16):
        for z in range(4):
            for y in range(2):
                target = (section + (1 if y else -1)) % 16
                pairs.append((section * 8 + 2 * z + y, target * 8 + 2 * z + (y ^ cross)))
    return lax.ppermute(value, ("pipe", "dp"), pairs)


def on_device(
    layer_input,
    residual_after,
    upstream,
    segment_lengths,
    project_weight,
    output_weight,
    expand_weight,
    reduce_weight,
):
    rank = lax.axis_index("dp")
    place = jnp.stack([rank // 2, rank % 2]).astype(jnp.int32)
    project = project_weight[0, :, 0]
    output = output_weight[0, 0]
    expand = expand_weight[0].reshape(2 * FF, D)
    reduce = reduce_weight[0]

    (own0,) = stacked([(residual_after, 0), (upstream, 0)], place)
    blocks0 = gather_blocks(own0)
    own1, sent, kept = second_slot(
        residual_after,
        upstream,
        layer_input,
        place,
        [blocks0[0, 1], blocks0[1, 0], blocks0[3, 0]],
    )
    over1 = shift(own1, 0, 1)
    (later1,) = copies([own1], [blocks0[1, 1], blocks0[3, 1]])
    blocks1 = gather_blocks(later1, over1)
    sent_weights = copies([project, output], later1)
    projects = (project, shift(sent_weights[0], 0, 1))
    outputs = (output, shift(sent_weights[1], 0, 1))
    fed0 = feed_forward(
        place,
        [blocks0[key] for key in BLOCKS],
        expand,
        reduce,
        [sent_weights[1], over1],
        long=False,
    )
    far0 = shift(fed0[6], 1, 0), shift(fed0[7], -1, 0)
    fed1 = feed_forward(
        place,
        [blocks1[key] for key in BLOCKS],
        expand,
        reduce,
        [fed0[2], projects[1]],
    )
    far1 = shift(fed1[6], 1, 0), shift(fed1[7], -1, 0)
    near0, done = term_near((fed0[5], fed0[8]), far0, fed1[2], long=False)
    near1, done = term_near((fed1[5], fed1[8]), far1, [done, outputs[1]])
    (sum0,) = term_sum(fed0[4], near0, done, long=False)
    term0 = one_way(sum0, 1)
    expand_slope = gradient([fed0[3], fed1[3]], [fed0[0], fed1[0]], sum0, long=False)
    (sum1,) = term_sum(fed1[4], near1, [expand_slope, term0])
    term1 = one_way(sum1, 0)
    layers, norm = layer_pair(kept, shift(sent, 0, 1), place, sum1, long=False)
    norm_other = shift(norm, 0, 1)
    reduce_slope = gradient([fed0[2], fed1[2]], [fed0[1], fed1[1]], norm, long=False)
    column, sides = gather_column(norm, [reduce_slope, term1], True, long=False)
    back_middle, low = branch_middle(
        [(fed0[4], *near0, term0), (fed1[4], *near1, term1)],
        (own0, own1),
        (blocks0[0, 1], over1),
        place,
        reduce_slope,
    )
    sides_other = shift(sides, 0, 1)
    seen = attend(place, segment_lengths[0], column, projects, [low, norm_other])
    far_other = shift(seen[0], 0, 1)
    pieces, _ = gather_column(low, seen[3], False, long=False)
    back = attend_back(pieces, seen[1], seen[2], outputs, projects, seen[3], long=False)
    far = shift(back[5], 1, 0), shift(back[6], -1, 0)
    sent_back = shift(back[2], 0, 1)
    own_slope, sent_slope = output_terms(seen[3], back[0], back[1], long=False)
    near, done = term_near((back[4], back[7]), far, [sent_slope, sides_other], long=False)
    project_slope = project_gradient(
        [(norm, seen[0], sides), (norm_other, far_other, sides_other)],
        [back[1], sent_back],
        done,
    )
    keep, cross = back_input(back[3], near, layers, back_middle, place, project_slope)
    output_slope = output_sum(own_slope, shift(sent_slope, 0, 1), keep)
    keep, cross = hand_on(keep, 0), hand_on(cross, 1)
    low_side = place[1] == 0
    arriving = jnp.stack([jnp.where(low_side, keep, cross), jnp.where(low_side, cross, keep)])
    return (
        arriving[None],
        project_slope[None, :, None],
        output_slope[None, None],
        expand_slope.reshape(1, 2, FF, D),
        reduce_slope[None],
    )


def solution(mesh):
    return jax.shard_map(
        on_device,
        mesh=mesh,
        in_specs=(
            P("pipe", None, "dp", None),
            P("pipe", None, "dp", None),
            P("pipe", None, "dp", None),
            P("pipe", None, None),
            P("pipe", None, "dp", None),
            P("pipe", "dp", None, None),
            P("pipe", None, "dp", None),
            P("pipe", "dp", None),
        ),
        out_specs=(
            P("pipe", None, "dp", None),
            P("pipe", None, "dp", None),
            P("pipe", "dp", None, None),
            P("pipe", None, "dp", None),
            P("pipe", "dp", None),
        ),
        check_vma=False,
    )
```

```python
import functools

import jax
import jax.numpy as jnp
from jax import lax
from jax.experimental import pallas as pl
from jax.experimental.pallas import tpu as pltpu
from jax.sharding import PartitionSpec as P

EPSILON = 1e-06
D = 3584
BLOCK = 64
PAIR = 2 * BLOCK
TOKENS = 512
FF = 256
HEAD = 128
HEADS = 3 * HEAD
TILE = 512
TILES = D // TILE
BF16 = jnp.bfloat16
F32 = jnp.float32

ANY = pl.BlockSpec(memory_space=pl.ANY)
HBM = pl.BlockSpec(memory_space=pltpu.HBM)
VMEM = pl.BlockSpec(memory_space=pltpu.VMEM)
SMEM = pl.BlockSpec(memory_space=pltpu.SMEM)


def rms_scale(values):
    return lax.rsqrt(jnp.mean(values * values, axis=-1, keepdims=True) + EPSILON)


def norm_back(values, row_scale, incoming):
    cubed = row_scale * row_scale * row_scale
    return row_scale * incoming - values * cubed * jnp.mean(
        incoming * values, axis=-1, keepdims=True
    )


def dot_nn(left, right):
    return lax.dot_general(left, right, (((1,), (0,)), ((), ())), preferred_element_type=F32)


def dot_nt(left, right):
    return lax.dot_general(left, right, (((1,), (1,)), ((), ())), preferred_element_type=F32)


def dot_tn(left, right):
    return lax.dot_general(left, right, (((0,), (0,)), ((), ())), preferred_element_type=F32)


def shape(*dims, dtype=BF16):
    return jax.ShapeDtypeStruct(dims, dtype)


def params():
    return pltpu.CompilerParams(vmem_limit_bytes=62 * 1024 * 1024)


def cost(long=True):
    return pl.CostEstimate(
        flops=10**12 if long else 0, bytes_accessed=10**10 if long else 0, transcendentals=0
    )


def listed(earlier):
    return list(earlier) if isinstance(earlier, (list, tuple)) else [earlier]


def rows_at(start, count):
    if not isinstance(start, int):
        start = pl.multiple_of(start, BLOCK)
    return pl.ds(start, count)


def block_rows(dz, y):
    return rows_at((2 * dz + y) * BLOCK, BLOCK)


def shift(value, dz, dy):
    pairs = [(i, ((i // 2 + dz) % 4) * 2 + ((i % 2) ^ dy)) for i in range(8)]
    return lax.ppermute(value, "dp", pairs)


def one_way(value, source):
    return lax.ppermute(value, "dp", [(2 * z + source, 2 * z + 1 - source) for z in range(4)])


def split_loads(plan):
    halves = ([], [])
    for number, index, rows, buffer, at in plan:
        for n in range(rows // BLOCK):
            part = at // BLOCK + n
            start = index[-1].start + n * BLOCK
            found = (number, (*index[:-1], pl.ds(start, BLOCK)), BLOCK, buffer, part * BLOCK)
            halves[part].append(found)
    return halves[0] + halves[1]


def small(arrays, loads, outs, earlier, body=None, place=None, long=True, parts=1):
    earlier = listed(earlier)
    plans = [loads(0)] if place is None else [loads(0), loads(1)]
    if parts == 2:
        plans = [split_loads(plan) for plan in plans]
    total = len(plans[0])
    buffers = {}
    for number, _, rows, buffer, at in plans[0] + plans[-1]:
        old = buffers.get(buffer, ((0,), None))[0]
        dims = (max(old[0], at + rows), arrays[number].shape[-1])
        buffers[buffer] = (dims, arrays[number].dtype)
    for out, buffer in outs:
        buffers[buffer] = (out.shape, out.dtype)
    names = sorted(buffers)
    n_place = 0 if place is None else 1

    def kernel(*refs):
        sources = refs[n_place : n_place + len(arrays)]
        refs_left = refs[n_place + len(arrays) + len(earlier) :]
        targets = refs_left[: len(outs)]
        held = dict(zip(names, refs_left[len(outs) :]))
        in_sem, out_sem = refs[-2:]

        def copies_of(plan, part=None):
            chosen = list(enumerate(plan))
            if part is not None:
                chosen = chosen[part * total // parts : (part + 1) * total // parts]
            return [
                pltpu.make_async_copy(
                    sources[number].at[index],
                    held[buffer].at[pl.ds(at, rows)],
                    in_sem.at[n],
                )
                for n, (number, index, rows, buffer, at) in chosen
            ]

        if place is None:
            for copy in copies_of(plans[0]):
                copy.start()
        else:
            for y in range(2):

                @pl.when(refs[0][1] == y)
                def _(y=y):
                    for copy in copies_of(plans[y]):
                        copy.start()

        place_ref = None if place is None else refs[0]
        out_copies = []
        for part in range(parts):
            for copy in copies_of(plans[0], part):
                copy.wait()
            if body is not None and parts == 1:
                body(held, place_ref)
            elif body is not None:
                body(held, place_ref, pl.ds(part * BLOCK, BLOCK))
            for n, ((out, buffer), target) in enumerate(zip(outs, targets)):
                rows = pl.ds(0, out.shape[0])
                if parts == 2 and out.shape[0] == PAIR:
                    rows = pl.ds(part * BLOCK, BLOCK)
                elif part < parts - 1:
                    continue
                copy = pltpu.make_async_copy(
                    held[buffer].at[rows], target.at[rows], out_sem.at[n * parts + part]
                )
                copy.start()
                out_copies.append(copy)
        for copy in out_copies:
            copy.wait()

    return pl.pallas_call(
        kernel,
        out_shape=tuple(out for out, _ in outs),
        in_specs=[SMEM] * n_place + [HBM] * len(arrays) + [ANY] * len(earlier),
        out_specs=(HBM,) * len(outs),
        scratch_shapes=[pltpu.VMEM(*buffers[k]) for k in names]
        + [pltpu.SemaphoreType.DMA((total,)), pltpu.SemaphoreType.DMA((parts * len(outs),))],
        compiler_params=params(),
        cost_estimate=cost(long),
    )(*([] if place is None else [place]), *arrays, *earlier)


def first_rows(start, rows):
    return (pl.ds(start, rows),)


def wide(ref):
    return ref[...].astype(F32)


def stacked(arrays, earlier):
    def loads(_):
        return [(n, (0, slot), BLOCK, "all", n * BLOCK) for n, (_, slot) in enumerate(arrays)]

    outs = [(shape(len(arrays) * BLOCK, D), "all")]
    return small([array for array, _ in arrays], loads, outs, earlier)


def gather_blocks(own, over=None, down=False):
    over = shift(own, 0, 1) if over is None else over
    below = shift(own, 1, 0)
    above = shift(own, -1, 0)
    below_over = shift(over, 1, 0)
    above_over = shift(over, -1, 0)
    far = shift(below, 1, 0)
    far_over = shift(above_over, -1, 0)
    return {
        (0, 0): own,
        (0, 1): over,
        (1, 0): above,
        (1, 1): above_over,
        (2, 0): far,
        (2, 1): far_over,
        (3, 0): below,
        (3, 1): below_over,
    }


def gather_column(own, earlier, both, long=True):
    below, above = shift(own, 1, 0), shift(own, -1, 0)

    def loads(_):
        return [
            (0, first_rows(0, BLOCK), BLOCK, "a", 0),
            (1, first_rows(BLOCK, BLOCK), BLOCK, "b", 0),
            (1, first_rows(0, PAIR), PAIR, "sides", 0),
            (0, first_rows(0, PAIR), PAIR, "sides", PAIR),
        ][: 4 if both else 2]

    outs = [(shape(BLOCK, D), "a"), (shape(BLOCK, D), "b"), (shape(2 * PAIR, D), "sides")]
    made = small([below, above], loads, outs[: 3 if both else 2], earlier, long=long)
    return (own, above, shift(made[0], 1, 0), shift(made[1], -1, 0), below), made[-1]


def term_near(terms, far, earlier, long=True):
    def loads(_):
        return [
            (0, first_rows(0, PAIR), PAIR, "up", 0),
            (1, first_rows(0, PAIR), PAIR, "down", 0),
            (2, first_rows(0, BLOCK), BLOCK, "a", 0),
            (3, first_rows(0, BLOCK), BLOCK, "b", 0),
        ]

    def body(held, _):
        up, down = held["up"], held["down"]
        up[:BLOCK] = (up[:BLOCK].astype(F32) + wide(held["a"])).astype(BF16)
        down[BLOCK:] = (down[BLOCK:].astype(F32) + wide(held["b"])).astype(BF16)

    outs = [(shape(PAIR, D), "up"), (shape(PAIR, D), "down")]
    up, down = small([terms[0], terms[1], *far], loads, outs, earlier, body, long=long)
    return (shift(up, 1, 0), shift(down, -1, 0)), up


def term_sum(term, near, earlier, long=True):
    def loads(_):
        whole = first_rows(0, PAIR)
        return [(0, whole, PAIR, "a", 0), (1, whole, PAIR, "b", 0), (2, whole, PAIR, "c", 0)]

    def body(held, _):
        held["a"][...] = (wide(held["a"]) + wide(held["b"]) + wide(held["c"])).astype(BF16)

    return small([term, *near], loads, [(shape(PAIR, D), "a")], earlier, body, long=long)


def branch_middle(terms, own, over, place, earlier, long=True):
    count = len(terms[0])

    def loads(y):
        first, second = 2 * count + 2 * y, 2 * count + 2 * y + 1
        if y == 1:
            first, second = second, first
        found = [
            (count * y + n, first_rows(0, PAIR), PAIR, f"term{n}", 0) for n in range(count)
        ]
        return found + [
            (first, first_rows(0, BLOCK), BLOCK, "values", 0),
            (second, first_rows(0, BLOCK), BLOCK, "values", BLOCK),
            (first, first_rows(BLOCK, BLOCK), BLOCK, "coming", 0),
            (second, first_rows(BLOCK, BLOCK), BLOCK, "coming", BLOCK),
        ]

    def body(held, _, rows):
        part = lambda name: held[name][rows].astype(F32)
        total = sum(part(f"term{n}") for n in range(count))
        values = part("values")
        result = part("coming") + norm_back(values, rms_scale(values), total)
        held["wide"][rows] = result
        held["coming"][rows] = result.astype(BF16)

    outs = [(shape(PAIR, D, dtype=F32), "wide"), (shape(PAIR, D), "coming")]
    arrays = [*terms[0], *terms[1], own[0], over[0], own[1], over[1]]
    return small(arrays, loads, outs, earlier, body, place, long, 2)


def back_input(term, near, layers, back_middle, place, earlier):
    def loads(_):
        names = ("term", "up", "down", "values", "wide")
        return [(n, first_rows(0, PAIR), PAIR, name, 0) for n, name in enumerate(names)]

    def body(held, place_ref, rows):
        part = lambda name: held[name][rows].astype(F32)
        total = part("term") + part("up") + part("down")
        values = part("values")
        result = part("wide") + norm_back(values, rms_scale(values), total)
        result = result.astype(BF16)
        mine = place_ref[1] == rows.start // BLOCK

        @pl.when(mine)
        def _():
            held["keep"][...] = result

        @pl.when(jnp.logical_not(mine))
        def _():
            held["cross"][...] = result

    outs = [(shape(BLOCK, D), "keep"), (shape(BLOCK, D), "cross")]
    arrays = [term, *near, layers, back_middle]
    return small(arrays, loads, outs, earlier, body, place, True, 2)


def second_slot(residual, upstream, layer, weights, place, earlier):
    def loads(y):
        return [
            (0, (0, 1), BLOCK, "own", 0),
            (1, (0, 1), BLOCK, "own", BLOCK),
            (2, (0, 1 - y), BLOCK, "sent", 0),
            (2, (0, y), BLOCK, "kept", 0),
            (3, first_rows(0, D), D, "p", 0),
            (4, first_rows(0, HEAD), HEAD, "o", 0),
        ]

    outs = [(shape(PAIR, D), "own"), (shape(BLOCK, D), "sent"), (shape(BLOCK, D), "kept")]
    outs += [(shape(D, 3 * HEAD), "p"), (shape(HEAD, D), "o")]
    return small([residual, upstream, layer, *weights], loads, outs, earlier, None, place, False)


def copies(arrays, earlier):
    def loads(_):
        return [
            (n, first_rows(0, array.shape[0]), array.shape[0], f"copy{n}", 0)
            for n, array in enumerate(arrays)
        ]

    outs = [(shape(*array.shape), f"copy{n}") for n, array in enumerate(arrays)]
    return small(arrays, loads, outs, earlier, long=False)


def sum_and_pair(term, near, kept, other, place, earlier):
    def loads(y):
        whole = first_rows(0, PAIR)
        return [
            (0, whole, PAIR, "a", 0),
            (1, whole, PAIR, "b", 0),
            (2, whole, PAIR, "c", 0),
            (3, first_rows(0, BLOCK), BLOCK, "rows", y * BLOCK),
            (4, first_rows(0, BLOCK), BLOCK, "rows", (1 - y) * BLOCK),
        ]

    def body(held, _, rows):
        part = lambda name: held[name][rows].astype(F32)
        held["a"][rows] = (part("a") + part("b") + part("c")).astype(BF16)
        values = part("rows")
        held["norm"][rows] = (values * rms_scale(values)).astype(BF16)

    outs = [(shape(PAIR, D), "a"), (shape(PAIR, D), "rows"), (shape(PAIR, D), "norm")]
    return small([term, *near, kept, other], loads, outs, earlier, body, place, True, 2)


BLOCKS = [(dz, dy) for dz in range(4) for dy in range(2)]


PIECES = (shape(PAIR, D), shape(PAIR, D), shape(BLOCK, D), shape(BLOCK, D), shape(PAIR, D))
PIECE_ROWS = ((0, PAIR), (PAIR, PAIR), (2 * PAIR, BLOCK), (2 * PAIR + BLOCK, BLOCK), (3 * PAIR, PAIR))


def store_pieces(terms, targets, cols, sem, t):
    copies = []
    for k, target in enumerate(targets):
        copies.append(
            pltpu.make_async_copy(
                terms.at[pl.ds(*PIECE_ROWS[k]), cols], target.at[:, cols], sem.at[5 * t + k]
            )
        )
        copies[-1].start()
    return copies


def feed_kernel(count, skip, *refs):
    place, pieces, refs = refs[0], refs[1 : 1 + count], refs[1 + count :]
    expand_in, reduce_in, refs = refs[0], refs[1], refs[2 + skip :]
    norm_out, coming_out, hidden_out, pair_out, *refs = refs
    targets, refs = refs[:5], refs[5:]
    middle, coming, norm, terms, expand, reduce, in_sem, coming_sem, out_sem, term_sem = refs
    z, y = place[0], place[1]

    def piece(k, part):
        if count == 8:
            return pieces[k].at[pl.ds(part * BLOCK, BLOCK)]
        dz, dy = BLOCKS[k]
        return pieces[0].at[rows_at(((z + dz) & 3) * 2 * PAIR + dy * PAIR + part * BLOCK, BLOCK)]

    def load(part, target, sem):
        return [
            pltpu.make_async_copy(
                piece(k, part),
                target.at[block_rows(dz, y ^ dy)],
                sem.at[k],
            )
            for k, (dz, dy) in enumerate(BLOCKS)
        ]

    copies = load(0, middle, in_sem)
    expand_copy = pltpu.make_async_copy(expand_in, expand, in_sem.at[8])
    coming_copies = load(1, coming, coming_sem)
    reduce_copy = pltpu.make_async_copy(reduce_in, reduce, coming_sem.at[8])
    for copy in copies + [expand_copy] + coming_copies + [reduce_copy]:
        copy.start()
    for dz in range(4):
        copies[2 * dz].wait()
        copies[2 * dz + 1].wait()
        for side in range(2):
            rows = block_rows(dz, side)
            values = middle[rows, :].astype(F32)
            norm[rows, :] = (values * rms_scale(values)).astype(BF16)
    norm_copy = pltpu.make_async_copy(norm, norm_out, out_sem.at[0])
    norm_copy.start()
    expand_copy.wait()
    pre = dot_nt(norm[...], expand[...])
    for copy in coming_copies:
        copy.wait()
    coming_copy = pltpu.make_async_copy(coming, coming_out, out_sem.at[1])
    coming_copy.start()
    reduce_copy.wait()
    back_hidden = dot_nt(coming[...], reduce[...])
    gate_pre, up_pre = pre[:, :FF], pre[:, FF:]
    gate_sigmoid = jax.nn.sigmoid(gate_pre)
    silu = gate_pre * gate_sigmoid
    hidden_out[...] = (silu * up_pre).astype(BF16)
    back_gate = back_hidden * up_pre * gate_sigmoid * (1.0 + gate_pre * (1.0 - gate_sigmoid))
    pair_out[:, :FF] = back_gate.astype(BF16)
    pair_out[:, FF:] = (back_hidden * silu).astype(BF16)
    out_copies = [norm_copy, coming_copy]
    for t in range(TILES):
        cols = pl.ds(t * TILE, TILE)
        terms[:, cols] = dot_nn(pair_out[...], expand[:, cols]).astype(BF16)
        out_copies += store_pieces(terms, targets, cols, term_sem, t)
    for copy in out_copies:
        copy.wait()


def feed_forward(place, blocks, expand, reduce, earlier, long=True):
    rows, count, earlier = (TOKENS, D), len(blocks), listed(earlier)
    return pl.pallas_call(
        functools.partial(feed_kernel, count, len(earlier)),
        out_shape=(
            shape(*rows),
            shape(*rows),
            shape(TOKENS, FF),
            shape(TOKENS, 2 * FF),
            *PIECES,
        ),
        in_specs=[SMEM] + [HBM] * (2 + count) + [ANY] * len(earlier),
        out_specs=(HBM, HBM, VMEM, VMEM) + (HBM,) * 5,
        scratch_shapes=[pltpu.VMEM(rows, BF16)] * 4
        + [
            pltpu.VMEM((2 * FF, D), BF16),
            pltpu.VMEM((FF, D), BF16),
            pltpu.SemaphoreType.DMA((9,)),
            pltpu.SemaphoreType.DMA((9,)),
            pltpu.SemaphoreType.DMA((2,)),
            pltpu.SemaphoreType.DMA((5 * TILES,)),
        ],
        compiler_params=params(),
        cost_estimate=cost(long),
    )(place, *blocks, expand, reduce, *earlier)


def load_pieces(pieces, rows, sem):
    copies = [
        pltpu.make_async_copy(pieces[k], rows.at[pl.ds(*PIECE_ROWS[k])], sem.at[k])
        for k in range(5)
    ]
    for copy in copies:
        copy.start()
    return copies


def attend_kernel(*refs):
    (place, lengths), pieces, (project0, project1, *_) = refs[:2], refs[2:7], refs[7:11]
    far_out, heads_out, soft_out, attended_out = refs[11:15]
    norm, project, in_sem, project_sem, out_sem = refs[15:]
    z, y = place[0], place[1]
    project_copies = [
        pltpu.make_async_copy(project0, project.at[:, pl.ds(0, HEADS)], project_sem.at[0]),
        pltpu.make_async_copy(project1, project.at[:, pl.ds(HEADS, HEADS)], project_sem.at[1]),
    ]
    copies = load_pieces(pieces, norm, in_sem)
    for copy in project_copies:
        copy.start()
    for copy in copies + project_copies:
        copy.wait()
    heads_out[...] = dot_nn(norm[...], project[...]).astype(BF16)
    far_copy = pltpu.make_async_copy(norm.at[pl.ds(2 * PAIR, PAIR)], far_out, out_sem)
    far_copy.start()

    def position_of(dims, axis):
        index = lax.broadcasted_iota(jnp.int32, dims, axis)
        block = index >> 6
        return (((z + (block >> 1)) & 3) * 2 + (block & 1)) * BLOCK + (index & 63)

    def segment_of(position):
        end = lengths[y, 0]
        total = (position >= end).astype(jnp.int32)
        for k in (1, 2, 3):
            end = end + lengths[y, k]
            total = total + (position >= end).astype(jnp.int32)
        return total

    row, column = position_of((TOKENS, 1), 0), position_of((1, TOKENS), 1)
    allowed = (segment_of(row) == segment_of(column)) & (column <= row)
    for h in range(2):
        heads = heads_out[:, h * HEADS : (h + 1) * HEADS]
        query, key, value = heads[:, :HEAD], heads[:, HEAD : 2 * HEAD], heads[:, 2 * HEAD :]
        scores = dot_nt(query, key) * HEAD ** (-0.5)
        weights = jnp.where(allowed, jnp.exp(scores), 0.0)
        soft = weights / jnp.sum(weights, axis=-1, keepdims=True)
        soft_out[h] = soft
        attended = dot_nn(soft.astype(BF16), value).astype(BF16)
        attended_out[:, h * HEAD : (h + 1) * HEAD] = attended
    far_copy.wait()


def attend(place, lengths, pieces, projects, earlier, long=True):
    return pl.pallas_call(
        attend_kernel,
        out_shape=(
            shape(PAIR, D),
            shape(TOKENS, 2 * HEADS),
            shape(2, TOKENS, TOKENS, dtype=F32),
            shape(TOKENS, 2 * HEAD),
        ),
        in_specs=[SMEM, SMEM] + [HBM] * 7 + [ANY] * 2,
        out_specs=(HBM, VMEM, VMEM, VMEM),
        scratch_shapes=[
            pltpu.VMEM((TOKENS, D), BF16),
            pltpu.VMEM((D, 2 * HEADS), BF16),
            pltpu.SemaphoreType.DMA((5,)),
            pltpu.SemaphoreType.DMA((2,)),
            pltpu.SemaphoreType.DMA,
        ],
        compiler_params=params(),
        cost_estimate=cost(long),
    )(place, lengths, *pieces, *projects, *earlier)


def back_kernel(*refs):
    pieces, (heads_in, soft_in, out0, out1, project0, project1, _) = refs[:5], refs[5:12]
    middle_out, back0, back1, targets = *refs[12:15], refs[15:20]
    middle, terms, project, output, heads, soft_all, back, in_sem, sem, out_sem, term_sem = refs[20:]
    copies = load_pieces(pieces, middle, in_sem)
    side_copies = [
        pltpu.make_async_copy(out0, output.at[pl.ds(0, HEAD)], sem.at[0]),
        pltpu.make_async_copy(out1, output.at[pl.ds(HEAD, HEAD)], sem.at[1]),
        pltpu.make_async_copy(heads_in, heads, sem.at[2]),
        pltpu.make_async_copy(soft_in, soft_all, sem.at[3]),
        pltpu.make_async_copy(project0, project.at[:, pl.ds(0, HEADS)], sem.at[4]),
        pltpu.make_async_copy(project1, project.at[:, pl.ds(HEADS, HEADS)], sem.at[5]),
    ]
    for copy in side_copies:
        copy.start()
    for copy in copies + side_copies[:2]:
        copy.wait()
    back_attended_all = dot_nt(middle[...], output[...]).astype(BF16)
    for copy in side_copies[2:4]:
        copy.wait()
    for h in range(2):
        back_attended = back_attended_all[:, h * HEAD : (h + 1) * HEAD]
        start = h * HEADS
        query = heads[:, start : start + HEAD]
        key = heads[:, start + HEAD : start + 2 * HEAD]
        value = heads[:, start + 2 * HEAD : start + HEADS]
        soft = soft_all[h]
        back_soft = dot_nt(back_attended, value)
        centre = jnp.sum(soft * back_soft, axis=-1, keepdims=True)
        back_scores = (soft * (back_soft - centre) * HEAD ** (-0.5)).astype(BF16)
        back[:, start : start + HEAD] = dot_nn(back_scores, key).astype(BF16)
        back[:, start + HEAD : start + 2 * HEAD] = dot_tn(back_scores, query).astype(BF16)
        back[:, start + 2 * HEAD : start + HEADS] = dot_tn(
            soft.astype(BF16), back_attended
        ).astype(BF16)
    middle_copy = pltpu.make_async_copy(middle, middle_out, out_sem.at[0])
    back_copies = [
        pltpu.make_async_copy(back.at[:, pl.ds(0, HEADS)], back0, out_sem.at[1]),
        pltpu.make_async_copy(back.at[:, pl.ds(HEADS, HEADS)], back1, out_sem.at[2]),
    ]
    out_copies = [middle_copy, *back_copies]
    for copy in side_copies[4:]:
        copy.wait()
    for copy in out_copies:
        copy.start()
    for t in range(TILES):
        cols = pl.ds(t * TILE, TILE)
        terms[:, cols] = dot_nt(back[...], project[cols, :]).astype(BF16)
        out_copies += store_pieces(terms, targets, cols, term_sem, t)
    for copy in out_copies:
        copy.wait()


def attend_back(pieces, heads, soft, outputs, projects, earlier, long=True):
    back = shape(TOKENS, 3 * HEAD)
    return pl.pallas_call(
        back_kernel,
        out_shape=(shape(TOKENS, D), back, back, *PIECES),
        in_specs=[HBM] * 11 + [ANY],
        out_specs=(HBM,) * 8,
        scratch_shapes=[pltpu.VMEM((TOKENS, D), BF16)] * 2
        + [
            pltpu.VMEM((D, 2 * HEADS), BF16),
            pltpu.VMEM((2 * HEAD, D), BF16),
            pltpu.VMEM((TOKENS, 2 * HEADS), BF16),
            pltpu.VMEM((2, TOKENS, TOKENS), F32),
            pltpu.VMEM((TOKENS, 2 * HEADS), BF16),
            pltpu.SemaphoreType.DMA((5,)),
            pltpu.SemaphoreType.DMA((6,)),
            pltpu.SemaphoreType.DMA((3,)),
            pltpu.SemaphoreType.DMA((5 * TILES,)),
        ],
        compiler_params=params(),
        cost_estimate=cost(long),
    )(*pieces, heads, soft, *outputs, *projects, earlier)


def fixed(*dims):
    return pl.BlockSpec(dims, lambda t: (0, 0))


def column_tile(rows):
    return pl.BlockSpec((rows, TILE), lambda t: (0, t))


def row_tile(columns):
    return pl.BlockSpec((TILE, columns), lambda t: (t, 0))


def gradient(lefts, rights, earlier, flip=False, long=True):
    rows, columns = lefts[0].shape[1], rights[0].shape[1]
    earlier = listed(earlier)

    def kernel(left0, right0, left1, right1, *refs):
        total = dot_tn(left0[...], right0[...]) + dot_tn(left1[...], right1[...])
        refs[-1][...] = total.astype(BF16)

    if flip:
        left, right, out = column_tile(TOKENS), fixed(TOKENS, columns), row_tile(columns)
    else:
        left, right, out = fixed(TOKENS, rows), column_tile(TOKENS), column_tile(rows)
    return pl.pallas_call(
        kernel,
        grid=(TILES,),
        out_shape=shape(rows, columns),
        in_specs=[left, right, left, right] + [ANY] * len(earlier),
        out_specs=out,
        compiler_params=params(),
        cost_estimate=cost(long),
    )(lefts[0], rights[0], lefts[1], rights[1], *earlier)


def project_kernel(own0, far0, sides0, back0, own1, far1, sides1, back1, _, out):
    left0 = jnp.concatenate([own0[...], sides0[:PAIR], far0[...], sides0[PAIR:]])
    left1 = jnp.concatenate([own1[...], sides1[:PAIR], far1[...], sides1[PAIR:]])
    out[...] = (dot_tn(left0, back0[...]) + dot_tn(left1, back1[...])).astype(BF16)


def project_gradient(norms, backs, earlier):
    pair, sides, back = column_tile(PAIR), column_tile(2 * PAIR), fixed(TOKENS, 3 * HEAD)
    return pl.pallas_call(
        project_kernel,
        grid=(TILES,),
        out_shape=shape(D, 3 * HEAD),
        in_specs=[pair, pair, sides, back] * 2 + [ANY],
        out_specs=row_tile(3 * HEAD),
        compiler_params=params(),
        cost_estimate=cost(),
    )(*norms[0], backs[0], *norms[1], backs[1], earlier)


def output_kernel(attended, middle, _, own_out, other_out):
    total = dot_tn(attended[...], middle[...])
    own_out[...] = total[:HEAD]
    other_out[...] = total[HEAD:].astype(BF16)


def output_terms(attended, middle, earlier, long=True):
    return pl.pallas_call(
        output_kernel,
        grid=(TILES,),
        out_shape=(shape(HEAD, D, dtype=F32), shape(HEAD, D)),
        in_specs=[fixed(TOKENS, 2 * HEAD), column_tile(TOKENS), ANY],
        out_specs=(column_tile(HEAD), column_tile(HEAD)),
        compiler_params=params(),
        cost_estimate=cost(long),
    )(attended, middle, earlier)


def output_sum(own, other, earlier):
    def loads(_):
        whole = first_rows(0, HEAD)
        return [(0, whole, HEAD, "own", 0), (1, whole, HEAD, "other", 0)]

    def body(held, _):
        held["other"][...] = (held["own"][...] + wide(held["other"])).astype(BF16)

    return small([own, other], loads, [(shape(HEAD, D), "other")], earlier, body)[0]


def hand_on(value, cross):
    pairs = []
    for section in range(16):
        for z in range(4):
            for y in range(2):
                target = (section + (1 if y else -1)) % 16
                pairs.append((section * 8 + 2 * z + y, target * 8 + 2 * z + (y ^ cross)))
    return lax.ppermute(value, ("pipe", "dp"), pairs)


def on_device(
    layer_input,
    residual_after,
    upstream,
    segment_lengths,
    project_weight,
    output_weight,
    expand_weight,
    reduce_weight,
):
    rank = lax.axis_index("dp")
    place = jnp.stack([rank // 2, rank % 2]).astype(jnp.int32)
    project = project_weight[0, :, 0]
    output = output_weight[0, 0]
    expand = expand_weight[0].reshape(2 * FF, D)
    reduce = reduce_weight[0]

    (own0,) = stacked([(residual_after, 0), (upstream, 0)], place)
    blocks0 = gather_blocks(own0)
    own1, sent, kept, *sent_weights = second_slot(
        residual_after,
        upstream,
        layer_input,
        (project, output),
        place,
        [blocks0[0, 1], blocks0[1, 0], blocks0[3, 0]],
    )
    over1 = shift(own1, 0, 1)
    other = shift(sent, 0, 1)
    (later1,) = copies([own1], [blocks0[1, 1], blocks0[3, 1]])
    blocks1 = gather_blocks(later1, over1)
    projects = (project, shift(sent_weights[0], 0, 1))
    outputs = (output, shift(sent_weights[1], 0, 1))
    fed0 = feed_forward(
        place,
        [blocks0[key] for key in BLOCKS],
        expand,
        reduce,
        [later1, over1],
        long=False,
    )
    far0 = shift(fed0[6], 1, 0), shift(fed0[7], -1, 0)
    fed1 = feed_forward(
        place,
        [blocks1[key] for key in BLOCKS],
        expand,
        reduce,
        [fed0[2], projects[1]],
    )
    far1 = shift(fed1[6], 1, 0), shift(fed1[7], -1, 0)
    near0, done = term_near((fed0[5], fed0[8]), far0, [fed1[2], other], long=False)
    near1, done = term_near((fed1[5], fed1[8]), far1, [done, outputs[1]])
    (sum0,) = term_sum(fed0[4], near0, done, long=False)
    term0 = one_way(sum0, 1)
    expand_slope = gradient([fed0[3], fed1[3]], [fed0[0], fed1[0]], sum0, long=False)
    sum1, layers, norm = sum_and_pair(
        fed1[4], near1, kept, other, place, [expand_slope, term0]
    )
    term1 = one_way(sum1, 0)
    norm_other = shift(norm, 0, 1)
    reduce_slope = gradient([fed0[2], fed1[2]], [fed0[1], fed1[1]], norm, long=False)
    column, sides = gather_column(norm, [reduce_slope, term1], True, long=False)
    back_middle, low = branch_middle(
        [(fed0[4], *near0, term0), (fed1[4], *near1, term1)],
        (own0, own1),
        (blocks0[0, 1], over1),
        place,
        reduce_slope,
    )
    sides_other = shift(sides, 0, 1)
    seen = attend(place, segment_lengths[0], column, projects, [low, norm_other])
    far_other = shift(seen[0], 0, 1)
    pieces, _ = gather_column(low, seen[3], False, long=False)
    back = attend_back(pieces, seen[1], seen[2], outputs, projects, seen[3], long=False)
    far = shift(back[5], 1, 0), shift(back[6], -1, 0)
    sent_back = shift(back[2], 0, 1)
    own_slope, sent_slope = output_terms(seen[3], back[0], back[1], long=False)
    near, done = term_near((back[4], back[7]), far, [sent_slope, sides_other], long=False)
    project_slope = project_gradient(
        [(norm, seen[0], sides), (norm_other, far_other, sides_other)],
        [back[1], sent_back],
        done,
    )
    keep, cross = back_input(back[3], near, layers, back_middle, place, project_slope)
    output_slope = output_sum(own_slope, shift(sent_slope, 0, 1), keep)
    keep, cross = hand_on(keep, 0), hand_on(cross, 1)
    low_side = place[1] == 0
    arriving = jnp.stack([jnp.where(low_side, keep, cross), jnp.where(low_side, cross, keep)])
    return (
        arriving[None],
        project_slope[None, :, None],
        output_slope[None, None],
        expand_slope.reshape(1, 2, FF, D),
        reduce_slope[None],
    )


def solution(mesh):
    return jax.shard_map(
        on_device,
        mesh=mesh,
        in_specs=(
            P("pipe", None, "dp", None),
            P("pipe", None, "dp", None),
            P("pipe", None, "dp", None),
            P("pipe", None, None),
            P("pipe", None, "dp", None),
            P("pipe", "dp", None, None),
            P("pipe", None, "dp", None),
            P("pipe", "dp", None),
        ),
        out_specs=(
            P("pipe", None, "dp", None),
            P("pipe", None, "dp", None),
            P("pipe", "dp", None, None),
            P("pipe", None, "dp", None),
            P("pipe", "dp", None),
        ),
        check_vma=False,
    )
```

```python
import functools

import jax
import jax.numpy as jnp
from jax import lax
from jax.experimental import pallas as pl
from jax.experimental.pallas import tpu as pltpu
from jax.sharding import PartitionSpec as P

EPSILON = 1e-06
D = 3584
BLOCK = 64
PAIR = 2 * BLOCK
TOKENS = 512
FF = 256
HEAD = 128
HEADS = 3 * HEAD
TILE = 512
TILES = D // TILE
BF16 = jnp.bfloat16
F32 = jnp.float32

ANY = pl.BlockSpec(memory_space=pl.ANY)
HBM = pl.BlockSpec(memory_space=pltpu.HBM)
VMEM = pl.BlockSpec(memory_space=pltpu.VMEM)
SMEM = pl.BlockSpec(memory_space=pltpu.SMEM)


def rms_scale(values):
    return lax.rsqrt(jnp.mean(values * values, axis=-1, keepdims=True) + EPSILON)


def norm_back(values, row_scale, incoming):
    cubed = row_scale * row_scale * row_scale
    return row_scale * incoming - values * cubed * jnp.mean(
        incoming * values, axis=-1, keepdims=True
    )


def dot_nn(left, right):
    return lax.dot_general(left, right, (((1,), (0,)), ((), ())), preferred_element_type=F32)


def dot_nt(left, right):
    return lax.dot_general(left, right, (((1,), (1,)), ((), ())), preferred_element_type=F32)


def dot_tn(left, right):
    return lax.dot_general(left, right, (((0,), (0,)), ((), ())), preferred_element_type=F32)


def shape(*dims, dtype=BF16):
    return jax.ShapeDtypeStruct(dims, dtype)


def params():
    return pltpu.CompilerParams(vmem_limit_bytes=62 * 1024 * 1024)


def cost(long=True):
    return pl.CostEstimate(
        flops=10**12 if long else 0, bytes_accessed=10**10 if long else 0, transcendentals=0
    )


def listed(earlier):
    return list(earlier) if isinstance(earlier, (list, tuple)) else [earlier]


def rows_at(start, count):
    if not isinstance(start, int):
        start = pl.multiple_of(start, BLOCK)
    return pl.ds(start, count)


def block_rows(dz, y):
    return rows_at((2 * dz + y) * BLOCK, BLOCK)


def shift(value, dz, dy):
    pairs = [(i, ((i // 2 + dz) % 4) * 2 + ((i % 2) ^ dy)) for i in range(8)]
    return lax.ppermute(value, "dp", pairs)


def one_way(value, source):
    return lax.ppermute(value, "dp", [(2 * z + source, 2 * z + 1 - source) for z in range(4)])


def split_loads(plan):
    halves = ([], [])
    for number, index, rows, buffer, at in plan:
        for n in range(rows // BLOCK):
            part = at // BLOCK + n
            start = index[-1].start + n * BLOCK
            found = (number, (*index[:-1], pl.ds(start, BLOCK)), BLOCK, buffer, part * BLOCK)
            halves[part].append(found)
    return halves[0] + halves[1]


def small(arrays, loads, outs, earlier, body=None, place=None, long=True, parts=1):
    earlier = listed(earlier)
    plans = [loads(0)] if place is None else [loads(0), loads(1)]
    if parts == 2:
        plans = [split_loads(plan) for plan in plans]
    total = len(plans[0])
    buffers = {}
    for number, _, rows, buffer, at in plans[0] + plans[-1]:
        old = buffers.get(buffer, ((0,), None))[0]
        dims = (max(old[0], at + rows), arrays[number].shape[-1])
        buffers[buffer] = (dims, arrays[number].dtype)
    for out, buffer in outs:
        buffers[buffer] = (out.shape, out.dtype)
    names = sorted(buffers)
    n_place = 0 if place is None else 1

    def kernel(*refs):
        sources = refs[n_place : n_place + len(arrays)]
        refs_left = refs[n_place + len(arrays) + len(earlier) :]
        targets = refs_left[: len(outs)]
        held = dict(zip(names, refs_left[len(outs) :]))
        in_sem, out_sem = refs[-2:]

        def copies_of(plan, part=None):
            chosen = list(enumerate(plan))
            if part is not None:
                chosen = chosen[part * total // parts : (part + 1) * total // parts]
            return [
                pltpu.make_async_copy(
                    sources[number].at[index],
                    held[buffer].at[pl.ds(at, rows)],
                    in_sem.at[n],
                )
                for n, (number, index, rows, buffer, at) in chosen
            ]

        if place is None:
            for copy in copies_of(plans[0]):
                copy.start()
        else:
            for y in range(2):

                @pl.when(refs[0][1] == y)
                def _(y=y):
                    for copy in copies_of(plans[y]):
                        copy.start()

        place_ref = None if place is None else refs[0]
        out_copies = []
        for part in range(parts):
            for copy in copies_of(plans[0], part):
                copy.wait()
            if body is not None and parts == 1:
                body(held, place_ref)
            elif body is not None:
                body(held, place_ref, pl.ds(part * BLOCK, BLOCK))
            for n, ((out, buffer), target) in enumerate(zip(outs, targets)):
                rows = pl.ds(0, out.shape[0])
                if parts == 2 and out.shape[0] == PAIR:
                    rows = pl.ds(part * BLOCK, BLOCK)
                elif part < parts - 1:
                    continue
                copy = pltpu.make_async_copy(
                    held[buffer].at[rows], target.at[rows], out_sem.at[n * parts + part]
                )
                copy.start()
                out_copies.append(copy)
        for copy in out_copies:
            copy.wait()

    return pl.pallas_call(
        kernel,
        out_shape=tuple(out for out, _ in outs),
        in_specs=[SMEM] * n_place + [HBM] * len(arrays) + [ANY] * len(earlier),
        out_specs=(HBM,) * len(outs),
        scratch_shapes=[pltpu.VMEM(*buffers[k]) for k in names]
        + [pltpu.SemaphoreType.DMA((total,)), pltpu.SemaphoreType.DMA((parts * len(outs),))],
        compiler_params=params(),
        cost_estimate=cost(long),
    )(*([] if place is None else [place]), *arrays, *earlier)


def first_rows(start, rows):
    return (pl.ds(start, rows),)


def wide(ref):
    return ref[...].astype(F32)


def stacked(arrays, earlier):
    def loads(_):
        return [(n, (0, slot), BLOCK, "all", n * BLOCK) for n, (_, slot) in enumerate(arrays)]

    outs = [(shape(len(arrays) * BLOCK, D), "all")]
    return small([array for array, _ in arrays], loads, outs, earlier)


def gather_blocks(own, over=None, across=0):
    over = shift(own, 0, 1) if over is None else over
    below = shift(own, 1, 0)
    above = shift(own, -1, 0)
    below_over = shift(over, 1, 0)
    above_over = shift(over, -1, 0)
    if across == 1:
        far_over = shift(above_over, -1, 0)
        far = shift(far_over, 0, 1)
    elif across == 2:
        far = shift(below, 1, 0)
        far_over = shift(far, 0, 1)
    else:
        far = shift(below, 1, 0)
        far_over = shift(above_over, -1, 0)
    return {
        (0, 0): own,
        (0, 1): over,
        (1, 0): above,
        (1, 1): above_over,
        (2, 0): far,
        (2, 1): far_over,
        (3, 0): below,
        (3, 1): below_over,
    }


def gather_column(own, earlier, both, long=True):
    below, above = shift(own, 1, 0), shift(own, -1, 0)

    def loads(_):
        return [
            (0, first_rows(0, BLOCK), BLOCK, "a", 0),
            (1, first_rows(BLOCK, BLOCK), BLOCK, "b", 0),
            (1, first_rows(0, PAIR), PAIR, "sides", 0),
            (0, first_rows(0, PAIR), PAIR, "sides", PAIR),
        ][: 4 if both else 2]

    outs = [(shape(BLOCK, D), "a"), (shape(BLOCK, D), "b"), (shape(2 * PAIR, D), "sides")]
    made = small([below, above], loads, outs[: 3 if both else 2], earlier, long=long)
    return (own, above, shift(made[0], 1, 0), shift(made[1], -1, 0), below), made[-1]


def term_near(terms, far, earlier, long=True):
    def loads(_):
        return [
            (0, first_rows(0, PAIR), PAIR, "up", 0),
            (1, first_rows(0, PAIR), PAIR, "down", 0),
            (2, first_rows(0, BLOCK), BLOCK, "a", 0),
            (3, first_rows(0, BLOCK), BLOCK, "b", 0),
        ]

    def body(held, _, rows):
        name, extra = ("up", "a") if rows.start == 0 else ("down", "b")
        held[name][rows] = (held[name][rows].astype(F32) + wide(held[extra])).astype(BF16)

    outs = [(shape(PAIR, D), "up"), (shape(PAIR, D), "down")]
    arrays = [terms[0], terms[1], *far]
    up, down = small(arrays, loads, outs, earlier, body, None, long, 2)
    return (shift(up, 1, 0), shift(down, -1, 0)), up


def term_sum(term, near, earlier, passed=(), long=True):
    def loads(_):
        names = ("a", "b", "c", "copy")[: 3 + len(passed)]
        return [(n, first_rows(0, PAIR), PAIR, name, 0) for n, name in enumerate(names)]

    def body(held, _, rows):
        total = sum(held[name][rows].astype(F32) for name in "abc")
        held["a"][rows] = total.astype(BF16)

    outs = [(shape(PAIR, D), "a")] + [(shape(PAIR, D), "copy") for _ in passed]
    return small([term, *near, *passed], loads, outs, earlier, body, None, long, 2)


def branch_middle(terms, own, over, place, earlier, long=True):
    count = len(terms[0])

    def loads(y):
        first, second = 2 * count + 2 * y, 2 * count + 2 * y + 1
        if y == 1:
            first, second = second, first
        found = [
            (count * y + n, first_rows(0, PAIR), PAIR, f"term{n}", 0) for n in range(count)
        ]
        return found + [
            (first, first_rows(0, BLOCK), BLOCK, "values", 0),
            (second, first_rows(0, BLOCK), BLOCK, "values", BLOCK),
            (first, first_rows(BLOCK, BLOCK), BLOCK, "coming", 0),
            (second, first_rows(BLOCK, BLOCK), BLOCK, "coming", BLOCK),
        ]

    def body(held, _, rows):
        part = lambda name: held[name][rows].astype(F32)
        total = sum(part(f"term{n}") for n in range(count))
        values = part("values")
        result = part("coming") + norm_back(values, rms_scale(values), total)
        held["wide"][rows] = result
        held["coming"][rows] = result.astype(BF16)

    outs = [(shape(PAIR, D, dtype=F32), "wide"), (shape(PAIR, D), "coming")]
    arrays = [*terms[0], *terms[1], own[0], over[0], own[1], over[1]]
    return small(arrays, loads, outs, earlier, body, place, long, 2)


def back_input(term, near, layers, back_middle, place, earlier):
    def loads(_):
        names = ("term", "up", "down", "values", "wide")
        return [(n, first_rows(0, PAIR), PAIR, name, 0) for n, name in enumerate(names)]

    def body(held, place_ref, rows):
        part = lambda name: held[name][rows].astype(F32)
        total = part("term") + part("up") + part("down")
        values = part("values")
        result = part("wide") + norm_back(values, rms_scale(values), total)
        result = result.astype(BF16)
        mine = place_ref[1] == rows.start // BLOCK

        @pl.when(mine)
        def _():
            held["keep"][...] = result

        @pl.when(jnp.logical_not(mine))
        def _():
            held["cross"][...] = result

    outs = [(shape(BLOCK, D), "keep"), (shape(BLOCK, D), "cross")]
    arrays = [term, *near, layers, back_middle]
    return small(arrays, loads, outs, earlier, body, place, True, 2)


def second_slot(residual, upstream, layer, weights, place, earlier):
    def loads(y):
        return [
            (0, (0, 1), BLOCK, "own", 0),
            (1, (0, 1), BLOCK, "own", BLOCK),
            (2, (0, 1 - y), BLOCK, "sent", 0),
            (2, (0, y), BLOCK, "kept", 0),
            (3, first_rows(0, D), D, "p", 0),
            (4, first_rows(0, HEAD), HEAD, "o", 0),
        ]

    outs = [(shape(PAIR, D), "own"), (shape(BLOCK, D), "sent"), (shape(BLOCK, D), "kept")]
    outs += [(shape(D, 3 * HEAD), "p"), (shape(HEAD, D), "o")]
    return small([residual, upstream, layer, *weights], loads, outs, earlier, None, place, False)


def copies(arrays, earlier):
    def loads(_):
        return [
            (n, first_rows(0, array.shape[0]), array.shape[0], f"copy{n}", 0)
            for n, array in enumerate(arrays)
        ]

    outs = [(shape(*array.shape), f"copy{n}") for n, array in enumerate(arrays)]
    return small(arrays, loads, outs, earlier, long=False)


def layer_pair(kept, other, place, earlier, long=True):
    def loads(y):
        return [
            (0, first_rows(0, BLOCK), BLOCK, "rows", y * BLOCK),
            (1, first_rows(0, BLOCK), BLOCK, "rows", (1 - y) * BLOCK),
        ]

    def body(held, _):
        for start in (0, BLOCK):
            rows = pl.ds(start, BLOCK)
            values = held["rows"][rows].astype(F32)
            held["norm"][rows] = (values * rms_scale(values)).astype(BF16)

    outs = [(shape(PAIR, D), "rows"), (shape(PAIR, D), "norm")]
    return small([kept, other], loads, outs, earlier, body, place, long)


BLOCKS = [(dz, dy) for dz in range(4) for dy in range(2)]


PIECES = (shape(PAIR, D), shape(PAIR, D), shape(BLOCK, D), shape(BLOCK, D), shape(PAIR, D))
PIECE_ROWS = ((0, PAIR), (PAIR, PAIR), (2 * PAIR, BLOCK), (2 * PAIR + BLOCK, BLOCK), (3 * PAIR, PAIR))


def store_pieces(terms, targets, cols, sem, t):
    copies = []
    for k, target in enumerate(targets):
        copies.append(
            pltpu.make_async_copy(
                terms.at[pl.ds(*PIECE_ROWS[k]), cols], target.at[:, cols], sem.at[5 * t + k]
            )
        )
        copies[-1].start()
    return copies


def feed_kernel(count, skip, *refs):
    place, pieces, refs = refs[0], refs[1 : 1 + count], refs[1 + count :]
    expand_in, reduce_in, refs = refs[0], refs[1], refs[2 + skip :]
    norm_out, coming_out, hidden_out, pair_out, *refs = refs
    targets, refs = refs[:5], refs[5:]
    middle, coming, norm, terms, expand, reduce, in_sem, coming_sem, out_sem, term_sem = refs
    z, y = place[0], place[1]

    def piece(k, part):
        if count == 8:
            return pieces[k].at[pl.ds(part * BLOCK, BLOCK)]
        dz, dy = BLOCKS[k]
        return pieces[0].at[rows_at(((z + dz) & 3) * 2 * PAIR + dy * PAIR + part * BLOCK, BLOCK)]

    def load(part, target, sem):
        return [
            pltpu.make_async_copy(
                piece(k, part),
                target.at[block_rows(dz, y ^ dy)],
                sem.at[k],
            )
            for k, (dz, dy) in enumerate(BLOCKS)
        ]

    copies = load(0, middle, in_sem)
    expand_copy = pltpu.make_async_copy(expand_in, expand, in_sem.at[8])
    coming_copies = load(1, coming, coming_sem)
    reduce_copy = pltpu.make_async_copy(reduce_in, reduce, coming_sem.at[8])
    for copy in copies + [expand_copy] + coming_copies + [reduce_copy]:
        copy.start()
    for dz in range(4):
        copies[2 * dz].wait()
        copies[2 * dz + 1].wait()
        for side in range(2):
            rows = block_rows(dz, side)
            values = middle[rows, :].astype(F32)
            norm[rows, :] = (values * rms_scale(values)).astype(BF16)
    norm_copy = pltpu.make_async_copy(norm, norm_out, out_sem.at[0])
    norm_copy.start()
    expand_copy.wait()
    pre = dot_nt(norm[...], expand[...])
    for copy in coming_copies:
        copy.wait()
    coming_copy = pltpu.make_async_copy(coming, coming_out, out_sem.at[1])
    coming_copy.start()
    reduce_copy.wait()
    back_hidden = dot_nt(coming[...], reduce[...])
    gate_pre, up_pre = pre[:, :FF], pre[:, FF:]
    gate_sigmoid = jax.nn.sigmoid(gate_pre)
    silu = gate_pre * gate_sigmoid
    hidden_out[...] = (silu * up_pre).astype(BF16)
    back_gate = back_hidden * up_pre * gate_sigmoid * (1.0 + gate_pre * (1.0 - gate_sigmoid))
    pair_out[:, :FF] = back_gate.astype(BF16)
    pair_out[:, FF:] = (back_hidden * silu).astype(BF16)
    out_copies = [norm_copy, coming_copy]
    for t in range(TILES):
        cols = pl.ds(t * TILE, TILE)
        terms[:, cols] = dot_nn(pair_out[...], expand[:, cols]).astype(BF16)
        out_copies += store_pieces(terms, targets, cols, term_sem, t)
    for copy in out_copies:
        copy.wait()


def feed_forward(place, blocks, expand, reduce, earlier, long=True):
    rows, count, earlier = (TOKENS, D), len(blocks), listed(earlier)
    return pl.pallas_call(
        functools.partial(feed_kernel, count, len(earlier)),
        out_shape=(
            shape(*rows),
            shape(*rows),
            shape(TOKENS, FF),
            shape(TOKENS, 2 * FF),
            *PIECES,
        ),
        in_specs=[SMEM] + [HBM] * (2 + count) + [ANY] * len(earlier),
        out_specs=(HBM, HBM, VMEM, VMEM) + (HBM,) * 5,
        scratch_shapes=[pltpu.VMEM(rows, BF16)] * 4
        + [
            pltpu.VMEM((2 * FF, D), BF16),
            pltpu.VMEM((FF, D), BF16),
            pltpu.SemaphoreType.DMA((9,)),
            pltpu.SemaphoreType.DMA((9,)),
            pltpu.SemaphoreType.DMA((2,)),
            pltpu.SemaphoreType.DMA((5 * TILES,)),
        ],
        compiler_params=params(),
        cost_estimate=cost(long),
    )(place, *blocks, expand, reduce, *earlier)


def load_pieces(pieces, rows, sem):
    copies = [
        pltpu.make_async_copy(pieces[k], rows.at[pl.ds(*PIECE_ROWS[k])], sem.at[k])
        for k in range(5)
    ]
    for copy in copies:
        copy.start()
    return copies


def attend_kernel(*refs):
    (place, lengths), pieces, (project0, project1, *_) = refs[:2], refs[2:7], refs[7:11]
    far_out, heads_out, soft_out, attended_out = refs[11:15]
    norm, project, in_sem, project_sem, out_sem = refs[15:]
    z, y = place[0], place[1]
    project_copies = [
        pltpu.make_async_copy(project0, project.at[:, pl.ds(0, HEADS)], project_sem.at[0]),
        pltpu.make_async_copy(project1, project.at[:, pl.ds(HEADS, HEADS)], project_sem.at[1]),
    ]
    copies = load_pieces(pieces, norm, in_sem)
    for copy in project_copies:
        copy.start()
    for copy in copies + project_copies:
        copy.wait()
    heads_out[...] = dot_nn(norm[...], project[...]).astype(BF16)
    far_copy = pltpu.make_async_copy(norm.at[pl.ds(2 * PAIR, PAIR)], far_out, out_sem)
    far_copy.start()

    def position_of(dims, axis):
        index = lax.broadcasted_iota(jnp.int32, dims, axis)
        block = index >> 6
        return (((z + (block >> 1)) & 3) * 2 + (block & 1)) * BLOCK + (index & 63)

    def segment_of(position):
        end = lengths[y, 0]
        total = (position >= end).astype(jnp.int32)
        for k in (1, 2, 3):
            end = end + lengths[y, k]
            total = total + (position >= end).astype(jnp.int32)
        return total

    row, column = position_of((TOKENS, 1), 0), position_of((1, TOKENS), 1)
    allowed = (segment_of(row) == segment_of(column)) & (column <= row)
    for h in range(2):
        heads = heads_out[:, h * HEADS : (h + 1) * HEADS]
        query, key, value = heads[:, :HEAD], heads[:, HEAD : 2 * HEAD], heads[:, 2 * HEAD :]
        scores = dot_nt(query, key) * HEAD ** (-0.5)
        weights = jnp.where(allowed, jnp.exp(scores), 0.0)
        soft = weights / jnp.sum(weights, axis=-1, keepdims=True)
        soft_out[h] = soft
        attended = dot_nn(soft.astype(BF16), value).astype(BF16)
        attended_out[:, h * HEAD : (h + 1) * HEAD] = attended
    far_copy.wait()


def attend(place, lengths, pieces, projects, earlier, long=True):
    return pl.pallas_call(
        attend_kernel,
        out_shape=(
            shape(PAIR, D),
            shape(TOKENS, 2 * HEADS),
            shape(2, TOKENS, TOKENS, dtype=F32),
            shape(TOKENS, 2 * HEAD),
        ),
        in_specs=[SMEM, SMEM] + [HBM] * 7 + [ANY] * 2,
        out_specs=(HBM, VMEM, VMEM, VMEM),
        scratch_shapes=[
            pltpu.VMEM((TOKENS, D), BF16),
            pltpu.VMEM((D, 2 * HEADS), BF16),
            pltpu.SemaphoreType.DMA((5,)),
            pltpu.SemaphoreType.DMA((2,)),
            pltpu.SemaphoreType.DMA,
        ],
        compiler_params=params(),
        cost_estimate=cost(long),
    )(place, lengths, *pieces, *projects, *earlier)


def back_kernel(*refs):
    pieces, (heads_in, soft_in, out0, out1, project0, project1, _) = refs[:5], refs[5:12]
    middle_out, back0, back1, targets = *refs[12:15], refs[15:20]
    middle, terms, project, output, heads, soft_all, back, in_sem, sem, out_sem, term_sem = refs[20:]
    copies = load_pieces(pieces, middle, in_sem)
    side_copies = [
        pltpu.make_async_copy(out0, output.at[pl.ds(0, HEAD)], sem.at[0]),
        pltpu.make_async_copy(out1, output.at[pl.ds(HEAD, HEAD)], sem.at[1]),
        pltpu.make_async_copy(heads_in, heads, sem.at[2]),
        pltpu.make_async_copy(soft_in, soft_all, sem.at[3]),
        pltpu.make_async_copy(project0, project.at[:, pl.ds(0, HEADS)], sem.at[4]),
        pltpu.make_async_copy(project1, project.at[:, pl.ds(HEADS, HEADS)], sem.at[5]),
    ]
    for copy in side_copies:
        copy.start()
    for copy in copies + side_copies[:2]:
        copy.wait()
    back_attended_all = dot_nt(middle[...], output[...]).astype(BF16)
    for copy in side_copies[2:4]:
        copy.wait()
    for h in range(2):
        back_attended = back_attended_all[:, h * HEAD : (h + 1) * HEAD]
        start = h * HEADS
        query = heads[:, start : start + HEAD]
        key = heads[:, start + HEAD : start + 2 * HEAD]
        value = heads[:, start + 2 * HEAD : start + HEADS]
        soft = soft_all[h]
        back_soft = dot_nt(back_attended, value)
        centre = jnp.sum(soft * back_soft, axis=-1, keepdims=True)
        back_scores = (soft * (back_soft - centre) * HEAD ** (-0.5)).astype(BF16)
        back[:, start : start + HEAD] = dot_nn(back_scores, key).astype(BF16)
        back[:, start + HEAD : start + 2 * HEAD] = dot_tn(back_scores, query).astype(BF16)
        back[:, start + 2 * HEAD : start + HEADS] = dot_tn(
            soft.astype(BF16), back_attended
        ).astype(BF16)
    middle_copy = pltpu.make_async_copy(middle, middle_out, out_sem.at[0])
    back_copies = [
        pltpu.make_async_copy(back.at[:, pl.ds(0, HEADS)], back0, out_sem.at[1]),
        pltpu.make_async_copy(back.at[:, pl.ds(HEADS, HEADS)], back1, out_sem.at[2]),
    ]
    out_copies = [middle_copy, *back_copies]
    for copy in side_copies[4:]:
        copy.wait()
    for copy in out_copies:
        copy.start()
    for t in range(TILES):
        cols = pl.ds(t * TILE, TILE)
        terms[:, cols] = dot_nt(back[...], project[cols, :]).astype(BF16)
        out_copies += store_pieces(terms, targets, cols, term_sem, t)
    for copy in out_copies:
        copy.wait()


def attend_back(pieces, heads, soft, outputs, projects, earlier, long=True):
    back = shape(TOKENS, 3 * HEAD)
    return pl.pallas_call(
        back_kernel,
        out_shape=(shape(TOKENS, D), back, back, *PIECES),
        in_specs=[HBM] * 11 + [ANY],
        out_specs=(HBM,) * 8,
        scratch_shapes=[pltpu.VMEM((TOKENS, D), BF16)] * 2
        + [
            pltpu.VMEM((D, 2 * HEADS), BF16),
            pltpu.VMEM((2 * HEAD, D), BF16),
            pltpu.VMEM((TOKENS, 2 * HEADS), BF16),
            pltpu.VMEM((2, TOKENS, TOKENS), F32),
            pltpu.VMEM((TOKENS, 2 * HEADS), BF16),
            pltpu.SemaphoreType.DMA((5,)),
            pltpu.SemaphoreType.DMA((6,)),
            pltpu.SemaphoreType.DMA((3,)),
            pltpu.SemaphoreType.DMA((5 * TILES,)),
        ],
        compiler_params=params(),
        cost_estimate=cost(long),
    )(*pieces, heads, soft, *outputs, *projects, earlier)


def fixed(*dims):
    return pl.BlockSpec(dims, lambda t: (0, 0))


def column_tile(rows):
    return pl.BlockSpec((rows, TILE), lambda t: (0, t))


def row_tile(columns):
    return pl.BlockSpec((TILE, columns), lambda t: (t, 0))


def gradient(lefts, rights, earlier, flip=False, long=True):
    rows, columns = lefts[0].shape[1], rights[0].shape[1]
    earlier = listed(earlier)

    def kernel(left0, right0, left1, right1, *refs):
        total = dot_tn(left0[...], right0[...]) + dot_tn(left1[...], right1[...])
        refs[-1][...] = total.astype(BF16)

    if flip:
        left, right, out = column_tile(TOKENS), fixed(TOKENS, columns), row_tile(columns)
    else:
        left, right, out = fixed(TOKENS, rows), column_tile(TOKENS), column_tile(rows)
    return pl.pallas_call(
        kernel,
        grid=(TILES,),
        out_shape=shape(rows, columns),
        in_specs=[left, right, left, right] + [ANY] * len(earlier),
        out_specs=out,
        compiler_params=params(),
        cost_estimate=cost(long),
    )(lefts[0], rights[0], lefts[1], rights[1], *earlier)


def project_kernel(own0, far0, sides0, back0, own1, far1, sides1, back1, _, out):
    left0 = jnp.concatenate([own0[...], sides0[:PAIR], far0[...], sides0[PAIR:]])
    left1 = jnp.concatenate([own1[...], sides1[:PAIR], far1[...], sides1[PAIR:]])
    out[...] = (dot_tn(left0, back0[...]) + dot_tn(left1, back1[...])).astype(BF16)


def project_gradient(norms, backs, earlier):
    pair, sides, back = column_tile(PAIR), column_tile(2 * PAIR), fixed(TOKENS, 3 * HEAD)
    return pl.pallas_call(
        project_kernel,
        grid=(TILES,),
        out_shape=shape(D, 3 * HEAD),
        in_specs=[pair, pair, sides, back] * 2 + [ANY],
        out_specs=row_tile(3 * HEAD),
        compiler_params=params(),
        cost_estimate=cost(),
    )(*norms[0], backs[0], *norms[1], backs[1], earlier)


def output_kernel(attended, middle, _, own_out, other_out):
    total = dot_tn(attended[...], middle[...])
    own_out[...] = total[:HEAD]
    other_out[...] = total[HEAD:].astype(BF16)


def output_terms(attended, middle, earlier, long=True):
    return pl.pallas_call(
        output_kernel,
        grid=(TILES,),
        out_shape=(shape(HEAD, D, dtype=F32), shape(HEAD, D)),
        in_specs=[fixed(TOKENS, 2 * HEAD), column_tile(TOKENS), ANY],
        out_specs=(column_tile(HEAD), column_tile(HEAD)),
        compiler_params=params(),
        cost_estimate=cost(long),
    )(attended, middle, earlier)


def output_sum(own, other, earlier):
    def loads(_):
        whole = first_rows(0, HEAD)
        return [(0, whole, HEAD, "own", 0), (1, whole, HEAD, "other", 0)]

    def body(held, _):
        held["other"][...] = (held["own"][...] + wide(held["other"])).astype(BF16)

    return small([own, other], loads, [(shape(HEAD, D), "other")], earlier, body)[0]


def hand_on(value, cross):
    pairs = []
    for section in range(16):
        for z in range(4):
            for y in range(2):
                target = (section + (1 if y else -1)) % 16
                pairs.append((section * 8 + 2 * z + y, target * 8 + 2 * z + (y ^ cross)))
    return lax.ppermute(value, ("pipe", "dp"), pairs)


def on_device(
    layer_input,
    residual_after,
    upstream,
    segment_lengths,
    project_weight,
    output_weight,
    expand_weight,
    reduce_weight,
):
    rank = lax.axis_index("dp")
    place = jnp.stack([rank // 2, rank % 2]).astype(jnp.int32)
    project = project_weight[0, :, 0]
    output = output_weight[0, 0]
    expand = expand_weight[0].reshape(2 * FF, D)
    reduce = reduce_weight[0]

    (own0,) = stacked([(residual_after, 0), (upstream, 0)], reduce_weight)
    blocks0 = gather_blocks(own0)
    own1, sent, kept, *sent_weights = second_slot(
        residual_after,
        upstream,
        layer_input,
        (project, output),
        place,
        [blocks0[0, 1], blocks0[1, 0], blocks0[3, 0]],
    )
    over1 = shift(own1, 0, 1)
    other = shift(sent, 0, 1)
    (later1,) = copies([own1], [blocks0[1, 1], blocks0[3, 1]])
    blocks1 = gather_blocks(later1, over1)
    projects = (project, shift(sent_weights[0], 0, 1))
    outputs = (output, shift(sent_weights[1], 0, 1))
    fed0 = feed_forward(
        place,
        [blocks0[key] for key in BLOCKS],
        expand,
        reduce,
        [later1, over1],
        long=False,
    )
    far0 = shift(fed0[6], 1, 0), shift(fed0[7], -1, 0)
    fed1 = feed_forward(
        place,
        [blocks1[key] for key in BLOCKS],
        expand,
        reduce,
        [fed0[2], projects[1]],
    )
    far1 = shift(fed1[6], 1, 0), shift(fed1[7], -1, 0)
    near0, done = term_near((fed0[5], fed0[8]), far0, fed1[2], long=False)
    near1, done = term_near((fed1[5], fed1[8]), far1, done)
    layers, norm = layer_pair(kept, other, place, done, long=False)
    norm_other = shift(norm, 0, 1)
    (sum0,) = term_sum(fed0[4], near0, [norm, outputs[1]], long=False)
    term0 = one_way(sum0, 1)
    expand_slope = gradient([fed0[3], fed1[3]], [fed0[0], fed1[0]], sum0, long=False)
    sum1, later = term_sum(fed1[4], near1, expand_slope, [norm])
    term1 = one_way(sum1, 0)
    reduce_slope = gradient([fed0[2], fed1[2]], [fed0[1], fed1[1]], [sum1, term0], long=False)
    column, sides = gather_column(later, [reduce_slope, term1], True, long=False)
    back_middle, low = branch_middle(
        [(fed0[4], *near0, term0), (fed1[4], *near1, term1)],
        (own0, own1),
        (blocks0[0, 1], over1),
        place,
        reduce_slope,
    )
    sides_other = shift(sides, 0, 1)
    seen = attend(place, segment_lengths[0], column, projects, [low, norm_other])
    far_other = shift(seen[0], 0, 1)
    pieces, _ = gather_column(low, seen[3], False, long=False)
    back = attend_back(pieces, seen[1], seen[2], outputs, projects, seen[3], long=False)
    far = shift(back[5], 1, 0), shift(back[6], -1, 0)
    sent_back = shift(back[2], 0, 1)
    own_slope, sent_slope = output_terms(seen[3], back[0], back[1], long=False)
    near, done = term_near((back[4], back[7]), far, [sent_slope, sides_other], long=False)
    project_slope = project_gradient(
        [(norm, seen[0], sides), (norm_other, far_other, sides_other)],
        [back[1], sent_back],
        done,
    )
    keep, cross = back_input(back[3], near, layers, back_middle, place, project_slope)
    output_slope = output_sum(own_slope, shift(sent_slope, 0, 1), keep)
    keep, cross = hand_on(keep, 0), hand_on(cross, 1)
    low_side = place[1] == 0
    arriving = jnp.stack([jnp.where(low_side, keep, cross), jnp.where(low_side, cross, keep)])
    return (
        arriving[None],
        project_slope[None, :, None],
        output_slope[None, None],
        expand_slope.reshape(1, 2, FF, D),
        reduce_slope[None],
    )


def solution(mesh):
    return jax.shard_map(
        on_device,
        mesh=mesh,
        in_specs=(
            P("pipe", None, "dp", None),
            P("pipe", None, "dp", None),
            P("pipe", None, "dp", None),
            P("pipe", None, None),
            P("pipe", None, "dp", None),
            P("pipe", "dp", None, None),
            P("pipe", None, "dp", None),
            P("pipe", "dp", None),
        ),
        out_specs=(
            P("pipe", None, "dp", None),
            P("pipe", None, "dp", None),
            P("pipe", "dp", None, None),
            P("pipe", None, "dp", None),
            P("pipe", "dp", None),
        ),
        check_vma=False,
    )
```

```python
import functools

import jax
import jax.numpy as jnp
from jax import lax
from jax.experimental import pallas as pl
from jax.experimental.pallas import tpu as pltpu
from jax.sharding import PartitionSpec as P

EPSILON = 1e-06
D = 3584
BLOCK = 64
PAIR = 2 * BLOCK
TOKENS = 512
FF = 256
HEAD = 128
HEADS = 3 * HEAD
TILE = 512
TILES = D // TILE
BF16 = jnp.bfloat16
F32 = jnp.float32

ANY = pl.BlockSpec(memory_space=pl.ANY)
HBM = pl.BlockSpec(memory_space=pltpu.HBM)
VMEM = pl.BlockSpec(memory_space=pltpu.VMEM)
SMEM = pl.BlockSpec(memory_space=pltpu.SMEM)


def rms_scale(values):
    return lax.rsqrt(jnp.mean(values * values, axis=-1, keepdims=True) + EPSILON)


def norm_back(values, row_scale, incoming):
    cubed = row_scale * row_scale * row_scale
    return row_scale * incoming - values * cubed * jnp.mean(
        incoming * values, axis=-1, keepdims=True
    )


def dot_nn(left, right):
    return lax.dot_general(left, right, (((1,), (0,)), ((), ())), preferred_element_type=F32)


def dot_nt(left, right):
    return lax.dot_general(left, right, (((1,), (1,)), ((), ())), preferred_element_type=F32)


def dot_tn(left, right):
    return lax.dot_general(left, right, (((0,), (0,)), ((), ())), preferred_element_type=F32)


def shape(*dims, dtype=BF16):
    return jax.ShapeDtypeStruct(dims, dtype)


def params():
    return pltpu.CompilerParams(vmem_limit_bytes=62 * 1024 * 1024)


def cost(long=True):
    return pl.CostEstimate(
        flops=10**12 if long else 0, bytes_accessed=10**10 if long else 0, transcendentals=0
    )


def listed(earlier):
    return list(earlier) if isinstance(earlier, (list, tuple)) else [earlier]


def rows_at(start, count):
    if not isinstance(start, int):
        start = pl.multiple_of(start, BLOCK)
    return pl.ds(start, count)


def block_rows(dz, y):
    return rows_at((2 * dz + y) * BLOCK, BLOCK)


def shift(value, dz, dy):
    pairs = [(i, ((i // 2 + dz) % 4) * 2 + ((i % 2) ^ dy)) for i in range(8)]
    return lax.ppermute(value, "dp", pairs)


def one_way(value, source):
    return lax.ppermute(value, "dp", [(2 * z + source, 2 * z + 1 - source) for z in range(4)])


def split_loads(plan):
    halves = ([], [])
    for number, index, rows, buffer, at in plan:
        for n in range(rows // BLOCK):
            part = at // BLOCK + n
            start = index[-1].start + n * BLOCK
            found = (number, (*index[:-1], pl.ds(start, BLOCK)), BLOCK, buffer, part * BLOCK)
            halves[part].append(found)
    return halves[0] + halves[1]


def small(arrays, loads, outs, earlier, body=None, place=None, long=True, parts=1):
    earlier = listed(earlier)
    plans = [loads(0)] if place is None else [loads(0), loads(1)]
    if parts == 2:
        plans = [split_loads(plan) for plan in plans]
    total = len(plans[0])
    buffers = {}
    for number, _, rows, buffer, at in plans[0] + plans[-1]:
        old = buffers.get(buffer, ((0,), None))[0]
        dims = (max(old[0], at + rows), arrays[number].shape[-1])
        buffers[buffer] = (dims, arrays[number].dtype)
    for out, buffer in outs:
        buffers[buffer] = (out.shape, out.dtype)
    names = sorted(buffers)
    n_place = 0 if place is None else 1

    def kernel(*refs):
        sources = refs[n_place : n_place + len(arrays)]
        refs_left = refs[n_place + len(arrays) + len(earlier) :]
        targets = refs_left[: len(outs)]
        held = dict(zip(names, refs_left[len(outs) :]))
        in_sem, out_sem = refs[-2:]

        def copies_of(plan, part=None):
            chosen = list(enumerate(plan))
            if part is not None:
                chosen = chosen[part * total // parts : (part + 1) * total // parts]
            return [
                pltpu.make_async_copy(
                    sources[number].at[index],
                    held[buffer].at[pl.ds(at, rows)],
                    in_sem.at[n],
                )
                for n, (number, index, rows, buffer, at) in chosen
            ]

        if place is None:
            for copy in copies_of(plans[0]):
                copy.start()
        else:
            for y in range(2):

                @pl.when(refs[0][1] == y)
                def _(y=y):
                    for copy in copies_of(plans[y]):
                        copy.start()

        place_ref = None if place is None else refs[0]
        out_copies = []
        for part in range(parts):
            for copy in copies_of(plans[0], part):
                copy.wait()
            if body is not None and parts == 1:
                body(held, place_ref)
            elif body is not None:
                body(held, place_ref, pl.ds(part * BLOCK, BLOCK))
            for n, ((out, buffer), target) in enumerate(zip(outs, targets)):
                rows = pl.ds(0, out.shape[0])
                if parts == 2 and out.shape[0] == PAIR:
                    rows = pl.ds(part * BLOCK, BLOCK)
                elif part < parts - 1:
                    continue
                copy = pltpu.make_async_copy(
                    held[buffer].at[rows], target.at[rows], out_sem.at[n * parts + part]
                )
                copy.start()
                out_copies.append(copy)
        for copy in out_copies:
            copy.wait()

    return pl.pallas_call(
        kernel,
        out_shape=tuple(out for out, _ in outs),
        in_specs=[SMEM] * n_place + [HBM] * len(arrays) + [ANY] * len(earlier),
        out_specs=(HBM,) * len(outs),
        scratch_shapes=[pltpu.VMEM(*buffers[k]) for k in names]
        + [pltpu.SemaphoreType.DMA((total,)), pltpu.SemaphoreType.DMA((parts * len(outs),))],
        compiler_params=params(),
        cost_estimate=cost(long),
    )(*([] if place is None else [place]), *arrays, *earlier)


def first_rows(start, rows):
    return (pl.ds(start, rows),)


def wide(ref):
    return ref[...].astype(F32)


def stacked(arrays, earlier):
    def loads(_):
        return [(n, (0, slot), BLOCK, "all", n * BLOCK) for n, (_, slot) in enumerate(arrays)]

    outs = [(shape(len(arrays) * BLOCK, D), "all")]
    return small([array for array, _ in arrays], loads, outs, earlier)


def gather_blocks(own, over=None, across=0):
    over = shift(own, 0, 1) if over is None else over
    below = shift(own, 1, 0)
    above = shift(own, -1, 0)
    below_over = shift(over, 1, 0)
    above_over = shift(over, -1, 0)
    if across == 1:
        far_over = shift(above_over, -1, 0)
        far = shift(far_over, 0, 1)
    elif across == 2:
        far = shift(below, 1, 0)
        far_over = shift(far, 0, 1)
    else:
        far = shift(below, 1, 0)
        far_over = shift(above_over, -1, 0)
    return {
        (0, 0): own,
        (0, 1): over,
        (1, 0): above,
        (1, 1): above_over,
        (2, 0): far,
        (2, 1): far_over,
        (3, 0): below,
        (3, 1): below_over,
    }


def gather_column(own, earlier, both, long=True):
    below, above = shift(own, 1, 0), shift(own, -1, 0)

    def loads(_):
        return [
            (0, first_rows(0, BLOCK), BLOCK, "a", 0),
            (1, first_rows(BLOCK, BLOCK), BLOCK, "b", 0),
            (1, first_rows(0, PAIR), PAIR, "sides", 0),
            (0, first_rows(0, PAIR), PAIR, "sides", PAIR),
        ][: 4 if both else 2]

    outs = [(shape(BLOCK, D), "a"), (shape(BLOCK, D), "b"), (shape(2 * PAIR, D), "sides")]
    made = small([below, above], loads, outs[: 3 if both else 2], earlier, long=long)
    return (own, above, shift(made[0], 1, 0), shift(made[1], -1, 0), below), made[-1]


def term_near(terms, far, earlier, long=True):
    def loads(_):
        return [
            (0, first_rows(0, PAIR), PAIR, "up", 0),
            (1, first_rows(0, PAIR), PAIR, "down", 0),
            (2, first_rows(0, BLOCK), BLOCK, "a", 0),
            (3, first_rows(0, BLOCK), BLOCK, "b", 0),
        ]

    def body(held, _, rows):
        name, extra = ("up", "a") if rows.start == 0 else ("down", "b")
        held[name][rows] = (held[name][rows].astype(F32) + wide(held[extra])).astype(BF16)

    outs = [(shape(PAIR, D), "up"), (shape(PAIR, D), "down")]
    arrays = [terms[0], terms[1], *far]
    up, down = small(arrays, loads, outs, earlier, body, None, long, 2)
    return (shift(up, 1, 0), shift(down, -1, 0)), up


def term_sum(term, near, earlier, passed=(), long=True):
    def loads(_):
        names = ("a", "b", "c", "copy")[: 3 + len(passed)]
        return [(n, first_rows(0, PAIR), PAIR, name, 0) for n, name in enumerate(names)]

    def body(held, _, rows):
        total = sum(held[name][rows].astype(F32) for name in "abc")
        held["a"][rows] = total.astype(BF16)

    outs = [(shape(PAIR, D), "a")] + [(shape(PAIR, D), "copy") for _ in passed]
    return small([term, *near, *passed], loads, outs, earlier, body, None, long, 2)


def branch_middle(terms, own, over, place, earlier, long=True):
    count = len(terms[0])

    def loads(y):
        first, second = 2 * count + 2 * y, 2 * count + 2 * y + 1
        if y == 1:
            first, second = second, first
        found = [
            (count * y + n, first_rows(0, PAIR), PAIR, f"term{n}", 0) for n in range(count)
        ]
        return found + [
            (first, first_rows(0, BLOCK), BLOCK, "values", 0),
            (second, first_rows(0, BLOCK), BLOCK, "values", BLOCK),
            (first, first_rows(BLOCK, BLOCK), BLOCK, "coming", 0),
            (second, first_rows(BLOCK, BLOCK), BLOCK, "coming", BLOCK),
        ]

    def body(held, _, rows):
        part = lambda name: held[name][rows].astype(F32)
        total = sum(part(f"term{n}") for n in range(count))
        values = part("values")
        result = part("coming") + norm_back(values, rms_scale(values), total)
        held["wide"][rows] = result
        held["coming"][rows] = result.astype(BF16)

    outs = [(shape(PAIR, D, dtype=F32), "wide"), (shape(PAIR, D), "coming")]
    arrays = [*terms[0], *terms[1], own[0], over[0], own[1], over[1]]
    return small(arrays, loads, outs, earlier, body, place, long, 2)


def back_input(term, near, layers, back_middle, place, earlier):
    def loads(_):
        names = ("term", "up", "down", "values", "wide")
        return [(n, first_rows(0, PAIR), PAIR, name, 0) for n, name in enumerate(names)]

    def body(held, place_ref, rows):
        part = lambda name: held[name][rows].astype(F32)
        total = part("term") + part("up") + part("down")
        values = part("values")
        result = part("wide") + norm_back(values, rms_scale(values), total)
        result = result.astype(BF16)
        mine = place_ref[1] == rows.start // BLOCK

        @pl.when(mine)
        def _():
            held["keep"][...] = result

        @pl.when(jnp.logical_not(mine))
        def _():
            held["cross"][...] = result

    outs = [(shape(BLOCK, D), "keep"), (shape(BLOCK, D), "cross")]
    arrays = [term, *near, layers, back_middle]
    return small(arrays, loads, outs, earlier, body, place, True, 2)


def second_slot(residual, upstream, layer, weights, place, earlier):
    def loads(y):
        return [
            (0, (0, 1), BLOCK, "own", 0),
            (1, (0, 1), BLOCK, "own", BLOCK),
            (2, (0, 1 - y), BLOCK, "sent", 0),
            (2, (0, y), BLOCK, "kept", 0),
            (3, first_rows(0, D), D, "p", 0),
            (4, first_rows(0, HEAD), HEAD, "o", 0),
        ]

    outs = [(shape(PAIR, D), "own"), (shape(BLOCK, D), "sent"), (shape(BLOCK, D), "kept")]
    outs += [(shape(D, 3 * HEAD), "p"), (shape(HEAD, D), "o")]
    return small([residual, upstream, layer, *weights], loads, outs, earlier, None, place, False)


def copies(arrays, earlier):
    def loads(_):
        return [
            (n, first_rows(0, array.shape[0]), array.shape[0], f"copy{n}", 0)
            for n, array in enumerate(arrays)
        ]

    outs = [(shape(*array.shape), f"copy{n}") for n, array in enumerate(arrays)]
    return small(arrays, loads, outs, earlier, long=False)


def layer_pair(kept, other, place, earlier, long=True):
    def loads(y):
        return [
            (0, first_rows(0, BLOCK), BLOCK, "rows", y * BLOCK),
            (1, first_rows(0, BLOCK), BLOCK, "rows", (1 - y) * BLOCK),
        ]

    def body(held, _):
        for start in (0, BLOCK):
            rows = pl.ds(start, BLOCK)
            values = held["rows"][rows].astype(F32)
            held["norm"][rows] = (values * rms_scale(values)).astype(BF16)

    outs = [(shape(PAIR, D), "rows"), (shape(PAIR, D), "norm")]
    return small([kept, other], loads, outs, earlier, body, place, long)


BLOCKS = [(dz, dy) for dz in range(4) for dy in range(2)]


PIECES = (shape(PAIR, D), shape(PAIR, D), shape(BLOCK, D), shape(BLOCK, D), shape(PAIR, D))
PIECE_ROWS = ((0, PAIR), (PAIR, PAIR), (2 * PAIR, BLOCK), (2 * PAIR + BLOCK, BLOCK), (3 * PAIR, PAIR))


def store_pieces(terms, targets, cols, sem, t):
    copies = []
    for k, target in enumerate(targets):
        copies.append(
            pltpu.make_async_copy(
                terms.at[pl.ds(*PIECE_ROWS[k]), cols], target.at[:, cols], sem.at[5 * t + k]
            )
        )
        copies[-1].start()
    return copies


def feed_kernel(count, skip, *refs):
    place, pieces, refs = refs[0], refs[1 : 1 + count], refs[1 + count :]
    expand_in, reduce_in, refs = refs[0], refs[1], refs[2 + skip :]
    norm_out, coming_out, hidden_out, pair_out, *refs = refs
    targets, refs = refs[:5], refs[5:]
    middle, coming, norm, terms, expand, reduce, in_sem, coming_sem, out_sem, term_sem = refs
    z, y = place[0], place[1]

    def piece(k, part):
        if count == 8:
            return pieces[k].at[pl.ds(part * BLOCK, BLOCK)]
        dz, dy = BLOCKS[k]
        return pieces[0].at[rows_at(((z + dz) & 3) * 2 * PAIR + dy * PAIR + part * BLOCK, BLOCK)]

    def load(part, target, sem):
        return [
            pltpu.make_async_copy(
                piece(k, part),
                target.at[block_rows(dz, y ^ dy)],
                sem.at[k],
            )
            for k, (dz, dy) in enumerate(BLOCKS)
        ]

    copies = load(0, middle, in_sem)
    expand_copy = pltpu.make_async_copy(expand_in, expand, in_sem.at[8])
    coming_copies = load(1, coming, coming_sem)
    reduce_copy = pltpu.make_async_copy(reduce_in, reduce, coming_sem.at[8])
    for copy in copies + [expand_copy] + coming_copies + [reduce_copy]:
        copy.start()
    for dz in range(4):
        copies[2 * dz].wait()
        copies[2 * dz + 1].wait()
        for side in range(2):
            rows = block_rows(dz, side)
            values = middle[rows, :].astype(F32)
            norm[rows, :] = (values * rms_scale(values)).astype(BF16)
    norm_copy = pltpu.make_async_copy(norm, norm_out, out_sem.at[0])
    norm_copy.start()
    expand_copy.wait()
    pre = dot_nt(norm[...], expand[...])
    for copy in coming_copies:
        copy.wait()
    coming_copy = pltpu.make_async_copy(coming, coming_out, out_sem.at[1])
    coming_copy.start()
    reduce_copy.wait()
    back_hidden = dot_nt(coming[...], reduce[...])
    gate_pre, up_pre = pre[:, :FF], pre[:, FF:]
    gate_sigmoid = jax.nn.sigmoid(gate_pre)
    silu = gate_pre * gate_sigmoid
    hidden_out[...] = (silu * up_pre).astype(BF16)
    back_gate = back_hidden * up_pre * gate_sigmoid * (1.0 + gate_pre * (1.0 - gate_sigmoid))
    pair_out[:, :FF] = back_gate.astype(BF16)
    pair_out[:, FF:] = (back_hidden * silu).astype(BF16)
    out_copies = [norm_copy, coming_copy]
    for t in range(TILES):
        cols = pl.ds(t * TILE, TILE)
        terms[:, cols] = dot_nn(pair_out[...], expand[:, cols]).astype(BF16)
        out_copies += store_pieces(terms, targets, cols, term_sem, t)
    for copy in out_copies:
        copy.wait()


def feed_forward(place, blocks, expand, reduce, earlier, long=True):
    rows, count, earlier = (TOKENS, D), len(blocks), listed(earlier)
    return pl.pallas_call(
        functools.partial(feed_kernel, count, len(earlier)),
        out_shape=(
            shape(*rows),
            shape(*rows),
            shape(TOKENS, FF),
            shape(TOKENS, 2 * FF),
            *PIECES,
        ),
        in_specs=[SMEM] + [HBM] * (2 + count) + [ANY] * len(earlier),
        out_specs=(HBM, HBM, VMEM, VMEM) + (HBM,) * 5,
        scratch_shapes=[pltpu.VMEM(rows, BF16)] * 4
        + [
            pltpu.VMEM((2 * FF, D), BF16),
            pltpu.VMEM((FF, D), BF16),
            pltpu.SemaphoreType.DMA((9,)),
            pltpu.SemaphoreType.DMA((9,)),
            pltpu.SemaphoreType.DMA((2,)),
            pltpu.SemaphoreType.DMA((5 * TILES,)),
        ],
        compiler_params=params(),
        cost_estimate=cost(long),
    )(place, *blocks, expand, reduce, *earlier)


def load_pieces(pieces, rows, sem):
    copies = [
        pltpu.make_async_copy(pieces[k], rows.at[pl.ds(*PIECE_ROWS[k])], sem.at[k])
        for k in range(5)
    ]
    for copy in copies:
        copy.start()
    return copies


def attend_kernel(*refs):
    (place, lengths), pieces, (project0, project1, *_) = refs[:2], refs[2:7], refs[7:11]
    far_out, heads_out, soft_out, attended_out = refs[11:15]
    norm, project, in_sem, project_sem, out_sem = refs[15:]
    z, y = place[0], place[1]
    project_copies = [
        pltpu.make_async_copy(project0, project.at[:, pl.ds(0, HEADS)], project_sem.at[0]),
        pltpu.make_async_copy(project1, project.at[:, pl.ds(HEADS, HEADS)], project_sem.at[1]),
    ]
    copies = load_pieces(pieces, norm, in_sem)
    for copy in project_copies:
        copy.start()
    for copy in copies + project_copies:
        copy.wait()
    heads_out[...] = dot_nn(norm[...], project[...]).astype(BF16)
    far_copy = pltpu.make_async_copy(norm.at[pl.ds(2 * PAIR, PAIR)], far_out, out_sem)
    far_copy.start()

    def position_of(dims, axis):
        index = lax.broadcasted_iota(jnp.int32, dims, axis)
        block = index >> 6
        return (((z + (block >> 1)) & 3) * 2 + (block & 1)) * BLOCK + (index & 63)

    def segment_of(position):
        end = lengths[y, 0]
        total = (position >= end).astype(jnp.int32)
        for k in (1, 2, 3):
            end = end + lengths[y, k]
            total = total + (position >= end).astype(jnp.int32)
        return total

    row, column = position_of((TOKENS, 1), 0), position_of((1, TOKENS), 1)
    allowed = (segment_of(row) == segment_of(column)) & (column <= row)
    for h in range(2):
        heads = heads_out[:, h * HEADS : (h + 1) * HEADS]
        query, key, value = heads[:, :HEAD], heads[:, HEAD : 2 * HEAD], heads[:, 2 * HEAD :]
        scores = dot_nt(query, key) * HEAD ** (-0.5)
        weights = jnp.where(allowed, jnp.exp(scores), 0.0)
        soft = weights / jnp.sum(weights, axis=-1, keepdims=True)
        soft_out[h] = soft
        attended = dot_nn(soft.astype(BF16), value).astype(BF16)
        attended_out[:, h * HEAD : (h + 1) * HEAD] = attended
    far_copy.wait()


def attend(place, lengths, pieces, projects, earlier, long=True):
    return pl.pallas_call(
        attend_kernel,
        out_shape=(
            shape(PAIR, D),
            shape(TOKENS, 2 * HEADS),
            shape(2, TOKENS, TOKENS, dtype=F32),
            shape(TOKENS, 2 * HEAD),
        ),
        in_specs=[SMEM, SMEM] + [HBM] * 7 + [ANY] * 2,
        out_specs=(HBM, VMEM, VMEM, VMEM),
        scratch_shapes=[
            pltpu.VMEM((TOKENS, D), BF16),
            pltpu.VMEM((D, 2 * HEADS), BF16),
            pltpu.SemaphoreType.DMA((5,)),
            pltpu.SemaphoreType.DMA((2,)),
            pltpu.SemaphoreType.DMA,
        ],
        compiler_params=params(),
        cost_estimate=cost(long),
    )(place, lengths, *pieces, *projects, *earlier)


def back_kernel(*refs):
    pieces, (heads_in, soft_in, out0, out1, project0, project1, _) = refs[:5], refs[5:12]
    middle_out, back0, back1, targets = *refs[12:15], refs[15:20]
    middle, terms, project, output, heads, soft_all, back, in_sem, sem, out_sem, term_sem = refs[20:]
    copies = load_pieces(pieces, middle, in_sem)
    side_copies = [
        pltpu.make_async_copy(out0, output.at[pl.ds(0, HEAD)], sem.at[0]),
        pltpu.make_async_copy(out1, output.at[pl.ds(HEAD, HEAD)], sem.at[1]),
        pltpu.make_async_copy(heads_in, heads, sem.at[2]),
        pltpu.make_async_copy(soft_in, soft_all, sem.at[3]),
        pltpu.make_async_copy(project0, project.at[:, pl.ds(0, HEADS)], sem.at[4]),
        pltpu.make_async_copy(project1, project.at[:, pl.ds(HEADS, HEADS)], sem.at[5]),
    ]
    for copy in side_copies:
        copy.start()
    for copy in copies + side_copies[:2]:
        copy.wait()
    back_attended_all = dot_nt(middle[...], output[...]).astype(BF16)
    for copy in side_copies[2:4]:
        copy.wait()
    for h in range(2):
        back_attended = back_attended_all[:, h * HEAD : (h + 1) * HEAD]
        start = h * HEADS
        query = heads[:, start : start + HEAD]
        key = heads[:, start + HEAD : start + 2 * HEAD]
        value = heads[:, start + 2 * HEAD : start + HEADS]
        soft = soft_all[h]
        back_soft = dot_nt(back_attended, value)
        centre = jnp.sum(soft * back_soft, axis=-1, keepdims=True)
        back_scores = (soft * (back_soft - centre) * HEAD ** (-0.5)).astype(BF16)
        back[:, start : start + HEAD] = dot_nn(back_scores, key).astype(BF16)
        back[:, start + HEAD : start + 2 * HEAD] = dot_tn(back_scores, query).astype(BF16)
        back[:, start + 2 * HEAD : start + HEADS] = dot_tn(
            soft.astype(BF16), back_attended
        ).astype(BF16)
    middle_copy = pltpu.make_async_copy(middle, middle_out, out_sem.at[0])
    back_copies = [
        pltpu.make_async_copy(back.at[:, pl.ds(0, HEADS)], back0, out_sem.at[1]),
        pltpu.make_async_copy(back.at[:, pl.ds(HEADS, HEADS)], back1, out_sem.at[2]),
    ]
    out_copies = [middle_copy, *back_copies]
    for copy in side_copies[4:]:
        copy.wait()
    for copy in out_copies:
        copy.start()
    for t in range(TILES):
        cols = pl.ds(t * TILE, TILE)
        terms[:, cols] = dot_nt(back[...], project[cols, :]).astype(BF16)
        out_copies += store_pieces(terms, targets, cols, term_sem, t)
    for copy in out_copies:
        copy.wait()


def attend_back(pieces, heads, soft, outputs, projects, earlier, long=True):
    back = shape(TOKENS, 3 * HEAD)
    return pl.pallas_call(
        back_kernel,
        out_shape=(shape(TOKENS, D), back, back, *PIECES),
        in_specs=[HBM] * 11 + [ANY],
        out_specs=(HBM,) * 8,
        scratch_shapes=[pltpu.VMEM((TOKENS, D), BF16)] * 2
        + [
            pltpu.VMEM((D, 2 * HEADS), BF16),
            pltpu.VMEM((2 * HEAD, D), BF16),
            pltpu.VMEM((TOKENS, 2 * HEADS), BF16),
            pltpu.VMEM((2, TOKENS, TOKENS), F32),
            pltpu.VMEM((TOKENS, 2 * HEADS), BF16),
            pltpu.SemaphoreType.DMA((5,)),
            pltpu.SemaphoreType.DMA((6,)),
            pltpu.SemaphoreType.DMA((3,)),
            pltpu.SemaphoreType.DMA((5 * TILES,)),
        ],
        compiler_params=params(),
        cost_estimate=cost(long),
    )(*pieces, heads, soft, *outputs, *projects, earlier)


def fixed(*dims):
    return pl.BlockSpec(dims, lambda t: (0, 0))


def column_tile(rows):
    return pl.BlockSpec((rows, TILE), lambda t: (0, t))


def row_tile(columns):
    return pl.BlockSpec((TILE, columns), lambda t: (t, 0))


def gradient(lefts, rights, earlier, flip=False, long=True):
    rows, columns = lefts[0].shape[1], rights[0].shape[1]
    earlier = listed(earlier)

    def kernel(left0, right0, left1, right1, *refs):
        total = dot_tn(left0[...], right0[...]) + dot_tn(left1[...], right1[...])
        refs[-1][...] = total.astype(BF16)

    if flip:
        left, right, out = column_tile(TOKENS), fixed(TOKENS, columns), row_tile(columns)
    else:
        left, right, out = fixed(TOKENS, rows), column_tile(TOKENS), column_tile(rows)
    return pl.pallas_call(
        kernel,
        grid=(TILES,),
        out_shape=shape(rows, columns),
        in_specs=[left, right, left, right] + [ANY] * len(earlier),
        out_specs=out,
        compiler_params=params(),
        cost_estimate=cost(long),
    )(lefts[0], rights[0], lefts[1], rights[1], *earlier)


def project_kernel(own0, far0, sides0, back0, own1, far1, sides1, back1, _, out):
    left0 = jnp.concatenate([own0[...], sides0[:PAIR], far0[...], sides0[PAIR:]])
    left1 = jnp.concatenate([own1[...], sides1[:PAIR], far1[...], sides1[PAIR:]])
    out[...] = (dot_tn(left0, back0[...]) + dot_tn(left1, back1[...])).astype(BF16)


def project_gradient(norms, backs, earlier):
    pair, sides, back = column_tile(PAIR), column_tile(2 * PAIR), fixed(TOKENS, 3 * HEAD)
    return pl.pallas_call(
        project_kernel,
        grid=(TILES,),
        out_shape=shape(D, 3 * HEAD),
        in_specs=[pair, pair, sides, back] * 2 + [ANY],
        out_specs=row_tile(3 * HEAD),
        compiler_params=params(),
        cost_estimate=cost(),
    )(*norms[0], backs[0], *norms[1], backs[1], earlier)


def output_kernel(attended, middle, _, own_out, other_out):
    total = dot_tn(attended[...], middle[...])
    own_out[...] = total[:HEAD]
    other_out[...] = total[HEAD:].astype(BF16)


def output_terms(attended, middle, earlier, long=True):
    return pl.pallas_call(
        output_kernel,
        grid=(TILES,),
        out_shape=(shape(HEAD, D, dtype=F32), shape(HEAD, D)),
        in_specs=[fixed(TOKENS, 2 * HEAD), column_tile(TOKENS), ANY],
        out_specs=(column_tile(HEAD), column_tile(HEAD)),
        compiler_params=params(),
        cost_estimate=cost(long),
    )(attended, middle, earlier)


def output_sum(own, other, earlier):
    def loads(_):
        whole = first_rows(0, HEAD)
        return [(0, whole, HEAD, "own", 0), (1, whole, HEAD, "other", 0)]

    def body(held, _):
        held["other"][...] = (held["own"][...] + wide(held["other"])).astype(BF16)

    return small([own, other], loads, [(shape(HEAD, D), "other")], earlier, body)[0]


def hand_on(value, cross):
    pairs = []
    for section in range(16):
        for z in range(4):
            for y in range(2):
                target = (section + (1 if y else -1)) % 16
                pairs.append((section * 8 + 2 * z + y, target * 8 + 2 * z + (y ^ cross)))
    return lax.ppermute(value, ("pipe", "dp"), pairs)


def on_device(
    layer_input,
    residual_after,
    upstream,
    segment_lengths,
    project_weight,
    output_weight,
    expand_weight,
    reduce_weight,
):
    rank = lax.axis_index("dp")
    place = jnp.stack([rank // 2, rank % 2]).astype(jnp.int32)
    project = project_weight[0, :, 0]
    output = output_weight[0, 0]
    expand = expand_weight[0].reshape(2 * FF, D)
    reduce = reduce_weight[0]

    (own0,) = stacked([(residual_after, 0), (upstream, 0)], reduce_weight)
    blocks0 = gather_blocks(own0)
    own1, sent, kept, *sent_weights = second_slot(
        residual_after,
        upstream,
        layer_input,
        (project, output),
        place,
        [blocks0[0, 1], blocks0[1, 0], blocks0[3, 0]],
    )
    over1 = shift(own1, 0, 1)
    other = shift(sent, 0, 1)
    (later1,) = copies([own1], [blocks0[1, 1], blocks0[3, 1]])
    blocks1 = gather_blocks(later1, over1)
    projects = (project, shift(sent_weights[0], 0, 1))
    outputs = (output, shift(sent_weights[1], 0, 1))
    fed0 = feed_forward(
        place,
        [blocks0[key] for key in BLOCKS],
        expand,
        reduce,
        [later1, over1],
        long=False,
    )
    far0 = shift(fed0[6], 1, 0), shift(fed0[7], -1, 0)
    fed1 = feed_forward(
        place,
        [blocks1[key] for key in BLOCKS],
        expand,
        reduce,
        [fed0[2], projects[1]],
    )
    far1 = shift(fed1[6], 1, 0), shift(fed1[7], -1, 0)
    near0, done = term_near((fed0[5], fed0[8]), far0, fed1[2], long=False)
    near1, done = term_near((fed1[5], fed1[8]), far1, done)
    layers, norm = layer_pair(kept, other, place, done, long=False)
    norm_other = shift(norm, 0, 1)
    (sum0,) = term_sum(fed0[4], near0, [norm, outputs[1]], long=False)
    term0 = one_way(sum0, 1)
    expand_slope = gradient([fed0[3], fed1[3]], [fed0[0], fed1[0]], sum0, long=False)
    sum1, later = term_sum(fed1[4], near1, [expand_slope, norm_other], [norm])
    term1 = one_way(sum1, 0)
    reduce_slope = gradient([fed0[2], fed1[2]], [fed0[1], fed1[1]], [sum1, term0], long=False)
    column, sides = gather_column(later, [reduce_slope, term1], True, long=False)
    back_middle, low = branch_middle(
        [(fed0[4], *near0, term0), (fed1[4], *near1, term1)],
        (own0, own1),
        (blocks0[0, 1], over1),
        place,
        reduce_slope,
    )
    sides_other = shift(sides, 0, 1)
    seen = attend(place, segment_lengths[0], column, projects, [low, norm_other])
    far_other = shift(seen[0], 0, 1)
    pieces, _ = gather_column(low, seen[3], False, long=False)
    back = attend_back(pieces, seen[1], seen[2], outputs, projects, seen[3], long=False)
    far = shift(back[5], 1, 0), shift(back[6], -1, 0)
    sent_back = shift(back[2], 0, 1)
    own_slope, sent_slope = output_terms(seen[3], back[0], back[1], long=False)
    near, done = term_near((back[4], back[7]), far, [sent_slope, sides_other], long=False)
    project_slope = project_gradient(
        [(norm, seen[0], sides), (norm_other, far_other, sides_other)],
        [back[1], sent_back],
        done,
    )
    keep, cross = back_input(back[3], near, layers, back_middle, place, project_slope)
    output_slope = output_sum(own_slope, shift(sent_slope, 0, 1), keep)
    keep, cross = hand_on(keep, 0), hand_on(cross, 1)
    low_side = place[1] == 0
    arriving = jnp.stack([jnp.where(low_side, keep, cross), jnp.where(low_side, cross, keep)])
    return (
        arriving[None],
        project_slope[None, :, None],
        output_slope[None, None],
        expand_slope.reshape(1, 2, FF, D),
        reduce_slope[None],
    )


def solution(mesh):
    return jax.shard_map(
        on_device,
        mesh=mesh,
        in_specs=(
            P("pipe", None, "dp", None),
            P("pipe", None, "dp", None),
            P("pipe", None, "dp", None),
            P("pipe", None, None),
            P("pipe", None, "dp", None),
            P("pipe", "dp", None, None),
            P("pipe", None, "dp", None),
            P("pipe", "dp", None),
        ),
        out_specs=(
            P("pipe", None, "dp", None),
            P("pipe", None, "dp", None),
            P("pipe", "dp", None, None),
            P("pipe", None, "dp", None),
            P("pipe", "dp", None),
        ),
        check_vma=False,
    )
```
